512 devices in a mesh: pb: 32 (over z_hi, y, core), ka: 16 (over x, z_lo).
Axes of the slice: x: 4, y: 8, z: 8 (z_hi: 2, z_lo: 4; z = z_hi * 4 + z_lo), core: 2. Of those that a mesh axis runs over, the one named last changes fastest.
Arguments:
- single_track: bfloat16 [2048, 384], P('pb'), may hold values from -48 to 48
- pair_track: bfloat16 [2048, 2048, 128], P('pb', 'ka'), may hold values from -80 to 80
- token_mask: int32 [2048], P('ka'), may hold values 0 or 1
- out_cotangent: bfloat16 [2048, 384], P('pb'), may hold values from -6 to 6
- query_weight: bfloat16 [384, 384], P('ka'), may hold values from -0.3125 to 0.3125
- query_bias: bfloat16 [384], replicated, may hold values from -4 to 4
- key_weight: bfloat16 [384, 384], P('ka'), may hold values from -0.3125 to 0.3125
- value_weight: bfloat16 [384, 384], P('ka'), may hold values from -0.3125 to 0.3125
- gate_weight: bfloat16 [384, 384], P('ka'), may hold values from -0.3125 to 0.3125
- output_weight: bfloat16 [384, 384], P('ka'), may hold values from -0.3125 to 0.3125
- pair_weight: bfloat16 [128, 16], replicated, may hold values from -1.5 to 30.125
Outputs:
- attention_out: bfloat16 [2048, 384], P('pb')
- single_grad: bfloat16 [2048, 384], P('pb')
- pair_grad: bfloat16 [2048, 2048, 128], P('pb', 'ka')
The draws below stay inside these ranges and needn't reach their ends.
Inputs may be any that keep to these rules, and one draw needn't show every extreme that they name: `token_mask`: 1 marks a real token, 0 padding.
All inputs are finite; a program needn't handle non-finite values. No bound on the sum of `token_mask` on one device may be relied on, other than what follows from the above.
Results may differ from the reference program's by a relative error of at most 0.0103.
Values may be sent and summed in bfloat16 or wider, within the bound.
A program may use at most 64 MiB of HBM per device.

```python
import math
import jax
import jax.numpy as jnp
from jax import lax

D = 384
HEADS = 16
CP = 128
ROWS_DEV = 64
CROP = 2048
N_PB = 32


def draw_single_track(key, part):
    key = jax.random.fold_in(key, 11)
    key_list = jax.random.split(key, 4)
    channel_scale = jnp.exp(jax.random.uniform(key_list[0], (1, D), minval=math.log(0.3), maxval=math.log(3.0)))
    values = jax.random.normal(key_list[3], (CROP, D)) * channel_scale
    return jnp.clip(values, -48.0, 48.0).astype(jnp.bfloat16)


def draw_pair_track(key, part):
    key = jax.random.fold_in(key, 23)
    key_list = jax.random.split(key, 4)
    channel_scale = jnp.exp(jax.random.uniform(key_list[0], (CP,), minval=0.0, maxval=math.log(10.0)))
    cell_scale = jnp.exp(jax.random.uniform(key_list[1], (CROP, CROP, 1), minval=math.log(0.5), maxval=math.log(2.0)))
    values = jax.random.normal(key_list[3], (CROP, CROP, CP)) * channel_scale * cell_scale
    return jnp.clip(values, -80.0, 80.0).astype(jnp.bfloat16)


def draw_pair_weight(key, part):
    key = jax.random.fold_in(key, 37)
    return jnp.clip(0.25 * jax.random.normal(key, (CP, HEADS)), -1.5, 1.5).astype(jnp.bfloat16)


def plant(values, own_key, smallest, largest):
    extent = values.shape
    place = [jax.random.randint(jax.random.fold_in(own_key, axis), (), 0, extent[axis]) for axis in range(len(extent))]
    values = values.at[tuple(place)].set(smallest)
    longest = extent.index(max(extent))
    place[longest] = (place[longest] + 1) % extent[longest]
    return values.at[tuple(place)].set(largest)


def steps_of(key, shape, cuts, low, top_value):
    gain, own = 1.0, jax.random.fold_in(key, 6)
    for dim, shards_of in cuts:
        draws = jnp.exp(jax.random.uniform(jax.random.fold_in(own, dim), (shards_of,), jnp.float32, low / len(cuts), top_value / len(cuts)))
        gain = gain * jnp.repeat(draws, shape[dim] // shards_of).reshape([-1 if axis == dim else 1 for axis in range(len(shape))])
    return gain


def gaussian(rng, dims, scale, most, cuts=(), kind=jnp.bfloat16):
    drawn = jax.random.normal(rng, dims, jnp.float32) * scale
    if len(cuts) > 0:
        drawn = steps_of(rng, dims, cuts, -0.22, 0.18) * drawn
    return jnp.clip(drawn, min=-most, max=most).astype(kind)


def setup_inputs(seed: int = 0) -> dict:
    seeds = jax.random.split(jax.random.key(seed), 12)
    return {
        "single_track": draw_single_track(jax.random.fold_in(seeds[11], 71), 0),
        "pair_track": draw_pair_track(jax.random.fold_in(seeds[11], 71), 0),
        "token_mask": plant((jax.random.randint(seeds[2], (CROP,), 0, 8) < 7).astype(jnp.int32), jax.random.fold_in(seeds[2], 1), 0, 1),
        "out_cotangent": gaussian(seeds[3], (CROP, D), 1.0, 6.0, ((0, 32),)),
        "query_weight": gaussian(seeds[4], (D, D), D ** -0.5, 0.3125, ((0, 16),)),
        "query_bias": gaussian(seeds[5], (D,), 1.0, 4.0),
        "key_weight": gaussian(seeds[6], (D, D), D ** -0.5, 0.3125, ((0, 16),)),
        "value_weight": gaussian(seeds[7], (D, D), D ** -0.5, 0.3125, ((0, 16),)),
        "gate_weight": gaussian(seeds[8], (D, D), D ** -0.5, 0.3125, ((0, 16),)),
        "output_weight": gaussian(seeds[9], (D, D), D ** -0.5, 0.3125, ((0, 16),)),
        "pair_weight": draw_pair_weight(jax.random.fold_in(seeds[11], 71), 0),
    }


NORM_EPSILON = 1e-05
MASK_PENALTY = 1000000000.0
WIDE_TYPE = jnp.float32
NARROW_TYPE = jnp.bfloat16
HIGHEST = lax.Precision.HIGHEST

def normalize(values):
    widened = values.astype(WIDE_TYPE)
    centred = widened - lax.optimization_barrier(jnp.mean(widened, axis=-1, keepdims=True))
    inverse = lax.rsqrt(lax.optimization_barrier(jnp.mean(centred * centred, axis=-1, keepdims=True)) + NORM_EPSILON)
    return (centred * inverse, inverse)

def norm_back(gradient, normed, inverse):
    return inverse * (gradient - lax.optimization_barrier(jnp.mean(gradient, axis=-1, keepdims=True)) - normed * lax.optimization_barrier(jnp.mean(gradient * normed, axis=-1, keepdims=True)))

def exact_product(first_operand, weight_matrix):
    return jnp.dot(first_operand, weight_matrix.astype(WIDE_TYPE), precision=HIGHEST)

def narrowed(values):
    return lax.optimization_barrier(values.astype(NARROW_TYPE)).astype(WIDE_TYPE)

def reference(single_track, pair_track, token_mask, out_cotangent, query_weight, query_bias, key_weight, value_weight, gate_weight, output_weight, pair_weight):
    head_dim = D // HEADS
    score_scale = head_dim ** (-0.5)
    normed_single, single_inverse = normalize(single_track)
    attention_input = normed_single.astype(NARROW_TYPE)
    query_rows = (jnp.dot(attention_input, query_weight, preferred_element_type=WIDE_TYPE) + query_bias.astype(WIDE_TYPE)).astype(NARROW_TYPE)
    key_rows = jnp.dot(attention_input, key_weight, preferred_element_type=WIDE_TYPE).astype(NARROW_TYPE)
    value_rows = jnp.dot(attention_input, value_weight, preferred_element_type=WIDE_TYPE).astype(NARROW_TYPE)
    gate_value = jax.nn.sigmoid(jnp.dot(attention_input, gate_weight, preferred_element_type=WIDE_TYPE))
    query_heads = query_rows.astype(WIDE_TYPE).reshape(CROP, HEADS, head_dim)
    key_heads = key_rows.astype(WIDE_TYPE).reshape(CROP, HEADS, head_dim)
    value_heads = value_rows.astype(WIDE_TYPE).reshape(CROP, HEADS, head_dim)
    penalty = (token_mask.astype(WIDE_TYPE) - 1.0) * MASK_PENALTY
    weight_bias = pair_weight.astype(WIDE_TYPE)
    gated_grads = jnp.dot(out_cotangent, output_weight.T, preferred_element_type=WIDE_TYPE)

    def block_step(running, row_start):
        key_total, value_total = running
        pair_rows = lax.dynamic_slice_in_dim(pair_track, row_start, ROWS_DEV, 0)
        pair_normed, pair_inverse = normalize(pair_rows)
        pair_bias = jnp.einsum('ijc,ch->hij', pair_normed, weight_bias, precision=HIGHEST)
        block_queries = lax.dynamic_slice_in_dim(query_heads, row_start, ROWS_DEV, 0)
        logits = jnp.einsum('ihd,jhd->hij', block_queries, key_heads, precision=HIGHEST) * score_scale + pair_bias + penalty
        row_max = lax.optimization_barrier(jnp.max(logits, axis=-1, keepdims=True))
        exp_scores = jnp.exp(logits - row_max)
        totals = lax.optimization_barrier(jnp.sum(exp_scores, axis=-1))
        numerator = jnp.einsum('hij,jhd->ihd', narrowed(exp_scores), value_heads, precision=HIGHEST)
        attended = numerator / totals.T[:, :, None]
        attended_flat = attended.reshape(ROWS_DEV, D)
        gate_rows = lax.dynamic_slice_in_dim(gate_value, row_start, ROWS_DEV, 0)
        gated_values = (gate_rows * attended_flat).astype(NARROW_TYPE)
        out_rows = jnp.dot(gated_values, output_weight, preferred_element_type=WIDE_TYPE).astype(NARROW_TYPE)
        cotangent_rows = lax.dynamic_slice_in_dim(gated_grads, row_start, ROWS_DEV, 0)
        attended_grad = narrowed(gate_rows * cotangent_rows)
        gate_input_grad = cotangent_rows * attended_flat * gate_rows * (1.0 - gate_rows)
        grad_heads = attended_grad.reshape(ROWS_DEV, HEADS, head_dim)
        row_delta = lax.optimization_barrier(jnp.sum(grad_heads * attended, axis=-1))
        softmax_rows = exp_scores / totals[:, :, None]
        prob_grads = jnp.einsum('ihd,jhd->hij', grad_heads, value_heads, precision=HIGHEST)
        score_grad = softmax_rows * (prob_grads - row_delta.T[:, :, None])
        score_weights = narrowed(score_grad)
        query_grad = (jnp.einsum('hij,jhd->ihd', score_weights, key_heads, precision=HIGHEST) * score_scale).reshape(ROWS_DEV, D)
        key_total = key_total + (jnp.einsum('hij,ihd->jhd', score_weights, block_queries, precision=HIGHEST) * score_scale).reshape(CROP, D)
        value_total = value_total + jnp.einsum('hij,ihd->jhd', narrowed(softmax_rows), grad_heads, precision=HIGHEST).reshape(CROP, D)
        channel_grad = jnp.einsum('hij,ch->ijc', score_grad, weight_bias, precision=HIGHEST)
        pair_rows_grad = norm_back(channel_grad, pair_normed, pair_inverse).astype(NARROW_TYPE)
        return ((key_total, value_total), (out_rows, pair_rows_grad, query_grad, gate_input_grad))
    starts = jnp.arange(N_PB, dtype=jnp.int32) * ROWS_DEV
    zero_rows = jnp.zeros((CROP, D), WIDE_TYPE)
    (key_total, value_total), (out_blocks, pair_blocks, query_blocks, gate_blocks) = lax.scan(block_step, (zero_rows, zero_rows), starts)
    attention_out = out_blocks.reshape(CROP, D)
    pair_grad = pair_blocks.reshape(CROP, CROP, CP)
    input_grad = exact_product(query_blocks.reshape(CROP, D), query_weight.T) + exact_product(key_total, key_weight.T) + exact_product(value_total, value_weight.T) + exact_product(gate_blocks.reshape(CROP, D), gate_weight.T)
    single_grad = norm_back(input_grad, normed_single, single_inverse).astype(NARROW_TYPE)
    return (attention_out, single_grad, pair_grad)
```

```python
import functools

import jax
import jax.numpy as jnp
from jax import lax
from jax.experimental import pallas as pl
from jax.experimental.pallas import tpu as pltpu
from jax.sharding import PartitionSpec as P

MESH = pl.DeviceIdType.MESH
F32 = jnp.float32
BF16 = jnp.bfloat16
EPS = 1e-05
PENALTY = 1000000000.0

ROWS = 64
COLS = 128
HEADS = 16
DIM = 24
D = 384
CP = 128
KA = 16
PB = 32
SCALE = DIM ** (-0.5)
K_T, Q_T, V_T, G_T, O_T = (0, 1, 2), (3, 4, 5), (8, 9, 10), (11, 12, 13), (6, 7, 14)
NEAR = [(a, b) for a in range(4) for b in ((0, 1, -1, 2) if a % 2 == 0 else (0, 1, -1, -2)) if (a, b) != (0, 0)]
NEAR.sort(key=lambda o: min(o[0], 4 - o[0]) + abs(o[1]))


def nt(a, b):
    return lax.dot_general(a, b, (((1,), (1,)), ((), ())), preferred_element_type=F32)


def tn(a, b):
    return lax.dot_general(a, b, (((0,), (0,)), ((), ())), preferred_element_type=F32)


def nn(a, b):
    return jnp.dot(a, b, preferred_element_type=F32)


def split2(v):
    hi = v.astype(BF16)
    return hi, (v - hi.astype(F32)).astype(BF16)


def kernel(
    single_ref, pair_hbm, mask_ref, ocot_ref, wq_ref, qb_ref, wk_ref, wv_ref, wg_ref, wo_ref, pw_ref,
    out_ref, sgrad_ref, pgrad_hbm,
    xp, nrm, invb, bias, sgp, a_i, nsg, isg, xall, wsend, wall, wfull, qbig, gbig, gate_s, cot_s,
    ebuf, dpbuf, sgb, pbb, stats, stat_send, kg_send, kg_recv, qg_send, qg_recv, fin_send, fin_recv, outb,
    in_sem, out_sem, x_ss, x_rs, w_ss, w_rs, f_ss, f_rs, s_ss, s_rs, k_ss, k_rs, q_ss, q_rs, o_ss, o_rs, loc_sem,
):
    p = lax.axis_index("pb")
    k = lax.axis_index("ka")
    core = lax.rem(p, 2)
    y = lax.rem(lax.div(p, 2), 8)
    x = lax.div(k, 4)
    z = lax.div(p, 16) * 4 + lax.rem(k, 4)
    sib = (p + 1 - 2 * core, k)
    own = lax.div(p, 2)
    quarter = lax.div(k, 4)
    rgroup = lax.rem(k, 4)

    def at(x2, z2):
        x2 = lax.rem(x2 + 4, 4)
        z2 = lax.rem(z2 + 8, 8)
        return ((lax.div(z2, 4) * 8 + y) * 2 + core, x2 * 4 + lax.rem(z2, 4))

    def ka_peer(o):
        return (p, lax.rem(k + o, KA))

    def x_target(o):
        return (quarter * 8 + lax.rem(p + o, 8), own)

    def x_source(o):
        return (2 * k + lax.div(o, 4), lax.div(p, 8) * 4 + lax.rem(o, 4))

    def pair_in(n):
        return pltpu.make_async_copy(pair_hbm.at[pl.ds(n * 16, 16)], xp.at[pl.ds(n * 16, 16)], in_sem.at[n])

    for n in range(4):
        pair_in(n).start()

    bar = pltpu.get_barrier_semaphore()
    for a, b in NEAR:
        pl.semaphore_signal(bar, inc=1, device_id=at(x - a, z - b), device_id_type=MESH)

    def greet_ka(o, c):
        pl.semaphore_signal(bar, inc=1, device_id=ka_peer(o), device_id_type=MESH)
        return c

    lax.fori_loop(1, KA, greet_ka, 0)
    pl.semaphore_signal(bar, inc=1, device_id=sib, device_id_type=MESH)

    def greet_x(o, c):
        src = x_source(o)

        @pl.when(jnp.logical_or(src[0] != p, src[1] != k))
        def _():
            pl.semaphore_signal(bar, inc=1, device_id=src, device_id_type=MESH)

        return c

    lax.fori_loop(0, 8, greet_x, 0)

    sv = single_ref[...].astype(F32)
    cen = sv - jnp.mean(sv, axis=-1, keepdims=True)
    inv = lax.rsqrt(jnp.mean(cen * cen, axis=-1, keepdims=True) + EPS)
    normed = cen * inv
    nsg[...] = normed
    isg[...] = jnp.broadcast_to(inv, (ROWS, 128))
    a_i[...] = normed.astype(BF16).reshape(4, 16, D)

    for ref, tiles in ((wk_ref, K_T), (wq_ref, Q_T), (wv_ref, V_T), (wg_ref, G_T), (wo_ref, O_T)):
        for n, t in enumerate(tiles):
            wsend[t] = ref[:, n * 128 : (n + 1) * 128]
    wsend[15] = jnp.zeros((24, 128), BF16)
    wall[k] = wsend[...]

    self_x = own == k
    pl.semaphore_wait(bar, 15 + 15 + 1 + 8 - self_x.astype(jnp.int32))

    x_slot = lax.rem(p, 2) * 4 + rgroup

    def x_copy(o):
        return pltpu.make_async_remote_copy(
            src_ref=a_i.at[rgroup], dst_ref=xall.at[x_slot], send_sem=x_ss.at[o], recv_sem=x_rs,
            device_id=x_target(o), device_id_type=MESH)

    def x_self():
        return pltpu.make_async_copy(a_i.at[rgroup], xall.at[x_slot], x_rs)

    @pl.when(self_x)
    def _():
        x_self().start()

    @pl.when(jnp.logical_not(self_x))
    def _():
        x_copy(0).start()

    def x_send(o, c):
        x_copy(o).start()
        return c

    lax.fori_loop(1, 8, x_send, 0)

    half = pl.ds(core * 8, 8)

    def w_copy(o):
        a, b = NEAR[o]
        return pltpu.make_async_remote_copy(
            src_ref=wsend.at[half], dst_ref=wall.at[k, half], send_sem=w_ss.at[o], recv_sem=w_rs.at[o],
            device_id=at(x + a, z + b), device_id_type=MESH)

    for o in range(15):
        w_copy(o).start()

    pwv = pw_ref[...].astype(F32)
    pwt = pwv.T
    pwt_b = pwt.astype(BF16)

    def pair_body(i, c):
        v = xp[i].astype(F32)
        cv = v - jnp.mean(v, axis=-1, keepdims=True)
        iv = lax.rsqrt(jnp.mean(cv * cv, axis=-1, keepdims=True) + EPS)
        n = cv * iv
        nrm[i] = n
        invb[i] = jnp.broadcast_to(iv, (COLS, 128))
        hi = n.astype(BF16)
        r = n - hi.astype(F32)
        mid = r.astype(BF16)
        lo = (r - mid.astype(F32)).astype(BF16)
        bias[pl.ds(pl.multiple_of(i * 16, 16), 16), :] = nt(pwt_b, hi) + (nt(pwt_b, mid) + nt(pwt_b, lo))
        return c

    for n in range(4):
        pair_in(n).wait()
        lax.fori_loop(n * 16, (n + 1) * 16, pair_body, 0, unroll=2)

    def f_copy(o):
        a, b = NEAR[o]
        src = at(x - a, z - b)[1]
        return pltpu.make_async_remote_copy(
            src_ref=wall.at[src, half], dst_ref=wall.at[src, half], send_sem=f_ss.at[o], recv_sem=f_rs.at[o],
            device_id=sib, device_id_type=MESH)

    for o in range(15):
        w_copy(o).wait_recv()
        f_copy(o).start()

    pltpu.make_async_copy(xall, xall, x_rs).wait()
    for o in range(15):
        f_copy(o).wait_recv()

    for n, tiles in enumerate((K_T, Q_T, V_T, G_T, O_T)):
        for m, t in enumerate(tiles):
            wfull[n, :, m * 128 : (m + 1) * 128] = wall[:, t].astype(F32).reshape(D, 128).astype(BF16)

    keys_in = xall[...].reshape(COLS, D)
    rows_in = a_i[...].reshape(ROWS, D)
    keys = nn(keys_in, wfull[0]).astype(BF16)
    values = nn(keys_in, wfull[2]).astype(BF16)
    queries = (nn(rows_in, wfull[1]) + qb_ref[...].astype(F32).reshape(1, D)).astype(BF16)
    gate = jax.nn.sigmoid(nn(rows_in, wfull[3]))
    cot = nt(ocot_ref[...], wfull[4])
    gate_s[...] = gate
    cot_s[...] = cot
    agrad = (gate * cot).astype(BF16)

    lane_head = lax.div(lax.broadcasted_iota(jnp.int32, (1, D), 1), DIM)
    heads_f = [jnp.where(lane_head == h, 1.0, 0.0).astype(F32) for h in range(HEADS)]
    for h in range(HEADS):
        mask_b = heads_f[h].astype(BF16)
        qbig[h * ROWS : (h + 1) * ROWS, :] = queries * mask_b
        gbig[h * ROWS : (h + 1) * ROWS, :] = agrad * mask_b

    pen = (mask_ref[...].astype(F32).reshape(1, COLS) - 1.0) * PENALTY
    lane = lax.broadcasted_iota(jnp.int32, (8, 128), 1)
    pm = jnp.zeros((8, 128), F32)
    pt = jnp.zeros((8, 128), F32)
    pd = jnp.zeros((8, 128), F32)
    for h in range(HEADS):
        rows = slice(h * ROWS, (h + 1) * ROWS)
        logits = nt(qbig[rows, :], keys) * SCALE + bias[pl.ds(h, ROWS, stride=HEADS), :] + pen
        dp = nt(gbig[rows, :], values)
        mx = jnp.max(logits, axis=-1, keepdims=True)
        e = jnp.exp(logits - mx)
        ebuf[rows, :] = e
        dpbuf[rows, :] = dp
        tot = jnp.sum(e, axis=-1, keepdims=True)
        dd = jnp.sum(e * dp, axis=-1, keepdims=True)
        for g in range(8):
            here = lane == g * 16 + h
            s8 = slice(g * 8, g * 8 + 8)
            pm = jnp.where(here, mx[s8], pm)
            pt = jnp.where(here, tot[s8], pt)
            pd = jnp.where(here, dd[s8], pd)
    stat_send[0:8, :] = pm
    stat_send[8:16, :] = pt
    stat_send[16:24, :] = pd

    def s_copy(o):
        return pltpu.make_async_remote_copy(
            src_ref=stat_send, dst_ref=stats.at[k], send_sem=s_ss.at[o], recv_sem=s_rs,
            device_id=ka_peer(o), device_id_type=MESH)

    def s_start(o, c):
        s_copy(o).start()
        return c

    lax.fori_loop(1, KA, s_start, 0)
    pltpu.make_async_copy(stat_send, stats.at[k], s_rs).start()
    pltpu.make_async_copy(stats, stats, s_rs).wait()

    st = stats[...]
    all_m, all_t, all_d = st[:, 0:8], st[:, 8:16], st[:, 16:24]
    gm = jnp.max(all_m, axis=0)
    wts = jnp.exp(all_m - gm[None])
    gt = jnp.sum(wts * all_t, axis=0)
    gd = jnp.sum(wts * all_d, axis=0)
    coef = jnp.exp(pm - gm) / gt
    delta = gd / gt

    for h in range(HEADS):
        rows = slice(h * ROWS, (h + 1) * ROWS)
        cc = jnp.concatenate([jnp.broadcast_to(coef[:, g * 16 + h : g * 16 + h + 1], (8, 128)) for g in range(8)], axis=0)
        dc = jnp.concatenate([jnp.broadcast_to(delta[:, g * 16 + h : g * 16 + h + 1], (8, 128)) for g in range(8)], axis=0)
        prob = ebuf[rows, :] * cc
        sg = prob * (dpbuf[rows, :] - dc)
        sgp[pl.ds(h, ROWS, stride=HEADS), :] = sg
        sgb[rows, :] = sg.astype(BF16)
        pbb[rows, :] = prob.astype(BF16)

    kg = tn(sgb[...], qbig[...]) * SCALE
    vg = tn(pbb[...], gbig[...])
    for c in range(2):
        for t in range(8):
            r8 = slice(c * 64 + t * 8, c * 64 + t * 8 + 8)
            kg_send[c * 8 + t] = jnp.concatenate([kg[r8], vg[r8]], axis=0).astype(BF16)

    def k_dest(n):
        c, t = lax.div(n, 8), lax.rem(n, 8)
        return (2 * k + c, 2 * t + c)

    def k_copy(n):
        return pltpu.make_async_remote_copy(
            src_ref=kg_send.at[n], dst_ref=kg_recv.at[p], send_sem=k_ss.at[n], recv_sem=k_rs,
            device_id=k_dest(n), device_id_type=MESH)

    def k_start(n, c):
        d = k_dest(n)
        mine = jnp.logical_and(d[0] == p, d[1] == k)

        @pl.when(mine)
        def _():
            pltpu.make_async_copy(kg_send.at[n], kg_recv.at[p], k_rs).start()

        @pl.when(jnp.logical_not(mine))
        def _():
            k_copy(n).start()

        return c

    lax.fori_loop(0, 16, k_start, 0)

    qg = jnp.zeros((ROWS, D), F32)
    att = jnp.zeros((ROWS, D), F32)
    for h in range(HEADS):
        rows = slice(h * ROWS, (h + 1) * ROWS)
        qg = qg + nn(sgb[rows, :], keys) * heads_f[h]
        att = att + nn(pbb[rows, :], values) * heads_f[h]
    qg = qg * SCALE
    for t in range(8):
        r8 = slice(t * 8, t * 8 + 8)
        qg_send[t] = jnp.concatenate([qg[r8], att[r8]], axis=0).astype(BF16)

    def q_copy(t):
        return pltpu.make_async_remote_copy(
            src_ref=qg_send.at[t], dst_ref=qg_recv.at[k], send_sem=q_ss.at[t], recv_sem=q_rs,
            device_id=(p, 2 * t + core), device_id_type=MESH)

    def q_start(t, c):
        mine = 2 * t + core == k

        @pl.when(mine)
        def _():
            pltpu.make_async_copy(qg_send.at[t], qg_recv.at[k], q_rs).start()

        @pl.when(jnp.logical_not(mine))
        def _():
            q_copy(t).start()

        return c

    lax.fori_loop(0, 8, q_start, 0)

    wc = pwt - jnp.mean(pwt, axis=-1, keepdims=True)
    wc_hi, wc_lo = split2(wc)
    zero16 = jnp.zeros((16, 128), BF16)
    ones8 = jnp.where(lax.broadcasted_iota(jnp.int32, (16, 128), 0) < 2, 1.0, 0.0).astype(BF16)
    rhs = jnp.concatenate(
        [jnp.concatenate([wc_hi, wc_hi, wc_lo, zero16], axis=0), jnp.concatenate([zero16, zero16, zero16, ones8], axis=0)], axis=1)
    row16 = lax.broadcasted_iota(jnp.int32, (16, 128), 0)

    def grad_body(i, c):
        r16 = pl.ds(pl.multiple_of(i * 16, 16), 16)
        sg = sgp[r16, :]
        s = jnp.sum(sg * bias[r16, :], axis=0, keepdims=True) * (1.0 / CP)
        hi, lo = split2(sg)
        s_hi = s.astype(BF16).astype(F32)
        s2 = jnp.where(row16 == 0, s_hi, jnp.where(row16 == 1, s - s_hi, 0.0)).astype(BF16)
        lhs = jnp.concatenate([hi, lo, hi, s2], axis=0)
        both = tn(lhs, rhs)
        outb[i] = (invb[i] * (both[:, :128] - nrm[i] * both[:, 128:])).astype(BF16)
        return c

    def pair_out(n):
        return pltpu.make_async_copy(outb.at[pl.ds(n * 16, 16)], pgrad_hbm.at[pl.ds(n * 16, 16)], out_sem.at[n])

    for n in range(4):
        lax.fori_loop(n * 16, (n + 1) * 16, grad_body, 0, unroll=2)
        pair_out(n).start()

    is_red = lax.rem(k, 2) == core
    t_me = lax.div(k, 2)

    def o_copy(o):
        return pltpu.make_async_remote_copy(
            src_ref=fin_send, dst_ref=fin_recv.at[t_me], send_sem=o_ss.at[o], recv_sem=o_rs,
            device_id=ka_peer(o), device_id_type=MESH)

    @pl.when(is_red)
    def _():
        pltpu.make_async_copy(qg_recv, qg_recv, q_rs).wait()
        pltpu.make_async_copy(kg_recv, kg_recv, k_rs).wait()
        kv = jnp.sum(kg_recv[...].astype(F32), axis=0)
        qa = jnp.sum(qg_recv[...].astype(F32), axis=0)
        r8 = pl.ds(pl.multiple_of(t_me * 8, 8), 8)
        g8 = gate_s[r8, :]
        att8 = qa[8:16]
        gig = cot_s[r8, :] * att8 * g8 * (1.0 - g8)
        grads = (kv[0:8], qa[0:8], kv[8:16], gig)
        ig = jnp.zeros((8, D), F32)
        for n, gr in enumerate(grads):
            hi, lo = split2(gr)
            two = nt(jnp.concatenate([hi.astype(F32), lo.astype(F32)], axis=0).astype(BF16), wfull[n])
            ig = ig + (two[0:8] + two[8:16])
        n8 = nsg[r8, :]
        sgr = isg[r8, 0:1] * (
            ig - jnp.mean(ig, axis=-1, keepdims=True) - n8 * jnp.mean(ig * n8, axis=-1, keepdims=True))
        gated = g8 * att8
        ao = nn(jnp.concatenate([gated, gated], axis=0).astype(BF16), wfull[4])[0:8]
        fin_send[...] = jnp.concatenate([sgr, ao], axis=0).astype(BF16)

        def o_start(o, c):
            o_copy(o).start()
            return c

        lax.fori_loop(1, KA, o_start, 0)
        pltpu.make_async_copy(fin_send, fin_recv.at[t_me], o_rs).start()

    pltpu.make_async_copy(fin_recv, fin_recv, o_rs).wait()
    fin = fin_recv[...].astype(F32)
    sgrad_ref[...] = fin[:, 0:8].reshape(ROWS, D).astype(BF16)
    out_ref[...] = fin[:, 8:16].reshape(ROWS, D).astype(BF16)

    @pl.when(jnp.logical_not(self_x))
    def _():
        x_copy(0).wait_send()

    def x_done(o, c):
        x_copy(o).wait_send()
        return c

    lax.fori_loop(1, 8, x_done, 0)
    for o in range(15):
        w_copy(o).wait_send()
        f_copy(o).wait_send()

    def s_done(o, c):
        s_copy(o).wait_send()
        return c

    lax.fori_loop(1, KA, s_done, 0)

    def k_done(n, c):
        d = k_dest(n)

        @pl.when(jnp.logical_or(d[0] != p, d[1] != k))
        def _():
            k_copy(n).wait_send()

        return c

    lax.fori_loop(0, 16, k_done, 0)

    def q_done(t, c):
        @pl.when(2 * t + core != k)
        def _():
            q_copy(t).wait_send()

        return c

    lax.fori_loop(0, 8, q_done, 0)

    @pl.when(is_red)
    def _():
        def o_done(o, c):
            o_copy(o).wait_send()
            return c

        lax.fori_loop(1, KA, o_done, 0)

    for n in range(4):
        pair_out(n).wait()


def local(*args):
    vmem = pl.BlockSpec(memory_space=pltpu.VMEM)
    hbm = pl.BlockSpec(memory_space=pl.ANY)
    dma = pltpu.SemaphoreType.DMA
    big = (ROWS, COLS, CP)
    flat = (HEADS * ROWS, 128)
    return pl.pallas_call(
        kernel,
        out_shape=(
            jax.ShapeDtypeStruct((ROWS, D), BF16),
            jax.ShapeDtypeStruct((ROWS, D), BF16),
            jax.ShapeDtypeStruct(big, BF16),
        ),
        in_specs=[vmem, hbm] + [vmem] * 9,
        out_specs=(vmem, vmem, hbm),
        scratch_shapes=[
            pltpu.VMEM(big, BF16),
            pltpu.VMEM(big, F32),
            pltpu.VMEM(big, F32),
            pltpu.VMEM(flat, F32),
            pltpu.VMEM(flat, F32),
            pltpu.VMEM((4, 16, D), BF16),
            pltpu.VMEM((ROWS, D), F32),
            pltpu.VMEM((ROWS, 128), F32),
            pltpu.VMEM((8, 16, D), BF16),
            pltpu.VMEM((16, 24, 128), BF16),
            pltpu.VMEM((KA, 16, 24, 128), BF16),
            pltpu.VMEM((5, D, D), BF16),
            pltpu.VMEM((HEADS * ROWS, D), BF16),
            pltpu.VMEM((HEADS * ROWS, D), BF16),
            pltpu.VMEM((ROWS, D), F32),
            pltpu.VMEM((ROWS, D), F32),
            pltpu.VMEM(flat, F32),
            pltpu.VMEM(flat, F32),
            pltpu.VMEM(flat, BF16),
            pltpu.VMEM(flat, BF16),
            pltpu.VMEM((KA, 24, 128), F32),
            pltpu.VMEM((24, 128), F32),
            pltpu.VMEM((16, 16, D), BF16),
            pltpu.VMEM((PB, 16, D), BF16),
            pltpu.VMEM((8, 16, D), BF16),
            pltpu.VMEM((KA, 16, D), BF16),
            pltpu.VMEM((16, D), BF16),
            pltpu.VMEM((8, 16, D), BF16),
            pltpu.VMEM(big, BF16),
            dma((4,)), dma((4,)),
            dma((8,)), dma,
            dma((15,)), dma((15,)),
            dma((15,)), dma((15,)),
            dma((16,)), dma,
            dma((16,)), dma,
            dma((8,)), dma,
            dma((16,)), dma,
            dma,
        ],
        compiler_params=pltpu.CompilerParams(
            collective_id=0, has_side_effects=True, vmem_limit_bytes=48 * 1024 * 1024),
    )(*args)


def solution(mesh):
    in_specs = (
        P("pb", None), P("pb", "ka", None), P("ka"), P("pb", None), P("ka", None), P(),
        P("ka", None), P("ka", None), P("ka", None), P("ka", None), P(),
    )
    out_specs = (P("pb", None), P("pb", None), P("pb", "ka", None))
    return jax.shard_map(local, mesh=mesh, in_specs=in_specs, out_specs=out_specs, check_vma=False)
```

```python
import functools

import jax
import jax.numpy as jnp
from jax import lax
from jax.experimental import pallas as pl
from jax.experimental.pallas import tpu as pltpu
from jax.sharding import PartitionSpec as P

MESH = pl.DeviceIdType.MESH
F32 = jnp.float32
BF16 = jnp.bfloat16
EPS = 1e-05
PENALTY = 1000000000.0

ROWS = 64
COLS = 128
HEADS = 16
DIM = 24
D = 384
CP = 128
KA = 16
PB = 32
SCALE = DIM ** (-0.5)
K_T, Q_T, V_T, G_T, O_T = (0, 1, 2), (3, 4, 5), (8, 9, 10), (11, 12, 13), (6, 7, 14)
NEAR = [(a, b) for a in range(4) for b in ((0, 1, -1, 2) if a % 2 == 0 else (0, 1, -1, -2)) if (a, b) != (0, 0)]
NEAR.sort(key=lambda o: min(o[0], 4 - o[0]) + abs(o[1]))


def nt(a, b):
    return lax.dot_general(a, b, (((1,), (1,)), ((), ())), preferred_element_type=F32)


def tn(a, b):
    return lax.dot_general(a, b, (((0,), (0,)), ((), ())), preferred_element_type=F32)


def nn(a, b):
    return jnp.dot(a, b, preferred_element_type=F32)


def split2(v):
    hi = v.astype(BF16)
    return hi, (v - hi.astype(F32)).astype(BF16)


def kernel(
    single_hbm, pair_hbm, mask_hbm, ocot_hbm, wq_hbm, qb_hbm, wk_hbm, wv_hbm, wg_hbm, wo_hbm, pw_hbm,
    out_ref, sgrad_ref, pgrad_hbm,
    outb,    single_ref, mask_ref, ocot_ref, qb_ref, pw_ref, xp, nrm, invb, bias, sgp, a_i, nsg, isg, xall, wsend, wall, wfull, qbig, gbig, gate_s, cot_s,
    ebuf, dpbuf, sgb, pbb, stats, stat_send, kv_half, kv_other, kg_send, kg_recv, qg_send, qg_recv, fin_send, fin_recv,
    in_sem, out_sem, small_sem, wl_sem, x_ss, x_rs, xf_ss, xf_rs, w_ss, w_rs, f_ss, f_rs, s_ss, s_rs, h_ss, h_rs, k_ss, k_rs, q_ss, q_rs, o_ss, o_rs,
):
    p = lax.axis_index("pb")
    k = lax.axis_index("ka")
    core = lax.rem(p, 2)
    y = lax.rem(lax.div(p, 2), 8)
    x = lax.div(k, 4)
    z = lax.div(p, 16) * 4 + lax.rem(k, 4)
    sib = (p + 1 - 2 * core, k)
    own = lax.div(p, 2)
    quarter = lax.div(k, 4)
    rgroup = lax.rem(k, 4)
    chip = lax.div(p, 2)

    def at(x2, z2):
        x2 = lax.rem(x2 + 4, 4)
        z2 = lax.rem(z2 + 8, 8)
        return ((lax.div(z2, 4) * 8 + y) * 2 + core, x2 * 4 + lax.rem(z2, 4))

    def ka_peer(o):
        return (p, lax.rem(k + o, KA))

    def x_target(o):
        return (quarter * 8 + lax.rem(p + 2 * o, 8), own)

    def x_source(o):
        return (2 * k + core, lax.div(p, 8) * 4 + o)

    def pair_in(n):
        return pltpu.make_async_copy(pair_hbm.at[pl.ds(n * 16, 16)], xp.at[pl.ds(n * 16, 16)], in_sem.at[n])

    single_in = pltpu.make_async_copy(single_hbm, single_ref, small_sem.at[0])
    single_in.start()
    weights_in = [
        pltpu.make_async_copy(ref.at[:, pl.ds(n * 128, 128)], wsend.at[t], wl_sem.at[t])
        for ref, tiles in ((wk_hbm, K_T), (wq_hbm, Q_T), (wv_hbm, V_T), (wg_hbm, G_T), (wo_hbm, O_T))
        for n, t in enumerate(tiles)
    ]
    for copy in weights_in:
        copy.start()
    small_in = [
        pltpu.make_async_copy(src, dst, small_sem.at[n + 1])
        for n, (src, dst) in enumerate(((mask_hbm, mask_ref), (ocot_hbm, ocot_ref), (qb_hbm, qb_ref), (pw_hbm, pw_ref)))
    ]
    for copy in small_in:
        copy.start()
    for n in range(4):
        pair_in(n).start()

    bar = pltpu.get_barrier_semaphore()
    for a, b in NEAR:
        pl.semaphore_signal(bar, inc=1, device_id=at(x - a, z - b), device_id_type=MESH)

    def greet_ka(o, c):
        pl.semaphore_signal(bar, inc=1, device_id=ka_peer(o), device_id_type=MESH)
        return c

    lax.fori_loop(1, KA, greet_ka, 0)
    pl.semaphore_signal(bar, inc=1, device_id=sib, device_id_type=MESH)

    def greet_x(o, c):
        src = x_source(o)

        @pl.when(jnp.logical_or(src[0] != p, src[1] != k))
        def _():
            pl.semaphore_signal(bar, inc=1, device_id=src, device_id_type=MESH)

        return c

    lax.fori_loop(0, 4, greet_x, 0)

    single_in.wait()
    sv = single_ref[...].astype(F32)
    cen = sv - jnp.mean(sv, axis=-1, keepdims=True)
    inv = lax.rsqrt(jnp.mean(cen * cen, axis=-1, keepdims=True) + EPS)
    normed = cen * inv
    nsg[...] = normed
    isg[...] = jnp.broadcast_to(inv, (ROWS, 128))
    a_i[...] = normed.astype(BF16).reshape(4, 16, D)

    for copy in weights_in:
        copy.wait()
    wsend[15] = jnp.zeros((24, 128), BF16)
    wall[k] = wsend[...]

    self_x = own == k
    pl.semaphore_wait(bar, 15 + 15 + 1 + 4 - self_x.astype(jnp.int32))

    def x_copy(o):
        return pltpu.make_async_remote_copy(
            src_ref=a_i.at[rgroup], dst_ref=xall.at[core, rgroup], send_sem=x_ss.at[o], recv_sem=x_rs,
            device_id=x_target(o), device_id_type=MESH)

    def x_self():
        return pltpu.make_async_copy(a_i.at[rgroup], xall.at[core, rgroup], x_rs)

    @pl.when(self_x)
    def _():
        x_self().start()

    @pl.when(jnp.logical_not(self_x))
    def _():
        x_copy(0).start()

    def x_send(o, c):
        x_copy(o).start()
        return c

    lax.fori_loop(1, 4, x_send, 0)

    half = pl.ds(core * 8, 8)

    def w_copy(o):
        a, b = NEAR[o]
        return pltpu.make_async_remote_copy(
            src_ref=wsend.at[half], dst_ref=wall.at[k, half], send_sem=w_ss.at[o], recv_sem=w_rs.at[o],
            device_id=at(x + a, z + b), device_id_type=MESH)

    for o in range(15):
        w_copy(o).start()

    for copy in small_in:
        copy.wait()
    pwt_b = pw_ref[...]
    pwt = pwt_b.astype(F32)

    mean_w = jnp.full((CP, CP), 1.0 / CP, BF16)

    def pair_body(n, c):
        i8 = pl.ds(pl.multiple_of(n * 8, 8), 8)
        vb = xp[i8].reshape(8 * COLS, CP)
        v = vb.astype(F32)
        cv = v - nn(vb, mean_w)
        sq_hi, sq_lo = split2(cv * cv)
        iv = lax.rsqrt(nn(sq_hi, mean_w) + nn(sq_lo, mean_w) + EPS)
        nv = cv * iv
        nrm[i8] = nv.reshape(8, COLS, CP)
        invb[i8] = iv.reshape(8, COLS, CP)
        hi, mid = split2(nv)
        both = nt(pwt_b, hi) + nt(pwt_b, mid)
        for m in range(8):
            bias[pl.ds(pl.multiple_of(n * 128 + m * 16, 16), 16), :] = both[:, m * 128 : (m + 1) * 128]
        return c

    for n in range(4):
        pair_in(n).wait()
        lax.fori_loop(n * 2, n * 2 + 2, pair_body, 0)

    def f_copy(o):
        a, b = NEAR[o]
        src = at(x - a, z - b)[1]
        return pltpu.make_async_remote_copy(
            src_ref=wall.at[src, half], dst_ref=wall.at[src, half], send_sem=f_ss.at[o], recv_sem=f_rs.at[o],
            device_id=sib, device_id_type=MESH)

    for o in range(15):
        w_copy(o).wait_recv()
        f_copy(o).start()

    pltpu.make_async_copy(xall.at[core], xall.at[core], x_rs).wait()
    x_fwd = pltpu.make_async_remote_copy(
        src_ref=xall.at[core], dst_ref=xall.at[core], send_sem=xf_ss, recv_sem=xf_rs,
        device_id=sib, device_id_type=MESH)
    x_fwd.start()

    def build(first):
        for n in range(8):
            wfull[first + n] = wall[:, first + n].astype(F32).reshape(D, 128).astype(BF16)

    build(core * 8)
    for o in range(15):
        f_copy(o).wait_recv()
    build(8 - core * 8)
    x_fwd.wait_recv()

    def weight(tiles):
        return jnp.concatenate([wfull[t] for t in tiles], axis=1)

    keys_in = xall[...].reshape(COLS, D)
    rows_in = a_i[...].reshape(ROWS, D)
    keys = nn(keys_in, weight(K_T)).astype(BF16)
    values = nn(keys_in, weight(V_T)).astype(BF16)
    queries = (nn(rows_in, weight(Q_T)) + qb_ref[...].astype(F32).reshape(1, D)).astype(BF16)
    gate = jax.nn.sigmoid(nn(rows_in, weight(G_T)))
    cot = nt(ocot_ref[...], weight(O_T))
    gate_s[...] = gate
    cot_s[...] = cot
    agrad = (gate * cot).astype(BF16)

    lane_head = lax.div(lax.broadcasted_iota(jnp.int32, (1, D), 1), DIM)
    heads_f = [jnp.where(lane_head == h, 1.0, 0.0).astype(F32) for h in range(HEADS)]
    for h in range(HEADS):
        mask_b = heads_f[h].astype(BF16)
        qbig[h * ROWS : (h + 1) * ROWS, :] = queries * mask_b
        gbig[h * ROWS : (h + 1) * ROWS, :] = agrad * mask_b

    pen = (mask_ref[...].astype(F32).reshape(1, COLS) - 1.0) * PENALTY
    lane = lax.broadcasted_iota(jnp.int32, (8, 128), 1)
    pm = jnp.zeros((8, 128), F32)
    pt = jnp.zeros((8, 128), F32)
    pd = jnp.zeros((8, 128), F32)
    for h in range(HEADS):
        rows = slice(h * ROWS, (h + 1) * ROWS)
        logits = nt(qbig[rows, :], keys) * SCALE + bias[pl.ds(h, ROWS, stride=HEADS), :] + pen
        dp = nt(gbig[rows, :], values)
        mx = jnp.max(logits, axis=-1, keepdims=True)
        e = jnp.exp(logits - mx)
        ebuf[rows, :] = e
        dpbuf[rows, :] = dp
        tot = jnp.sum(e, axis=-1, keepdims=True)
        dd = jnp.sum(e * dp, axis=-1, keepdims=True)
        for g in range(8):
            here = lane == g * 16 + h
            s8 = slice(g * 8, g * 8 + 8)
            pm = jnp.where(here, mx[s8], pm)
            pt = jnp.where(here, tot[s8], pt)
            pd = jnp.where(here, dd[s8], pd)
    stat_send[0:8, :] = pm
    stat_send[8:16, :] = pt
    stat_send[16:24, :] = pd

    def s_copy(o):
        return pltpu.make_async_remote_copy(
            src_ref=stat_send, dst_ref=stats.at[k], send_sem=s_ss.at[o], recv_sem=s_rs,
            device_id=ka_peer(o), device_id_type=MESH)

    def s_start(o, c):
        s_copy(o).start()
        return c

    lax.fori_loop(1, KA, s_start, 0)
    pltpu.make_async_copy(stat_send, stats.at[k], s_rs).start()
    num = jnp.zeros((ROWS, D), F32)
    for h in range(HEADS):
        rows = slice(h * ROWS, (h + 1) * ROWS)
        num = num + nn(ebuf[rows, :].astype(BF16), values) * heads_f[h]
    pltpu.make_async_copy(stats, stats, s_rs).wait()

    st = stats[...]
    all_m, all_t, all_d = st[:, 0:8], st[:, 8:16], st[:, 16:24]
    gm = jnp.max(all_m, axis=0)
    wts = jnp.exp(all_m - gm[None])
    gt = jnp.sum(wts * all_t, axis=0)
    gd = jnp.sum(wts * all_d, axis=0)
    coef = jnp.exp(pm - gm) / gt
    delta = gd / gt
    coef_f = jnp.zeros((ROWS, D), F32)

    for h in range(HEADS):
        rows = slice(h * ROWS, (h + 1) * ROWS)
        cc = jnp.concatenate([jnp.broadcast_to(coef[:, g * 16 + h : g * 16 + h + 1], (8, 128)) for g in range(8)], axis=0)
        dc = jnp.concatenate([jnp.broadcast_to(delta[:, g * 16 + h : g * 16 + h + 1], (8, 128)) for g in range(8)], axis=0)
        coef_f = coef_f + jnp.concatenate([cc] * 3, axis=1) * heads_f[h]
        prob = ebuf[rows, :] * cc
        sg = prob * (dpbuf[rows, :] - dc)
        sgp[pl.ds(h, ROWS, stride=HEADS), :] = sg
        sgb[rows, :] = sg.astype(BF16)
        pbb[rows, :] = prob.astype(BF16)

    att = num * coef_f

    def back(v, n):
        hi, lo = split2(v)
        w = weight(n)
        return nt(hi, w) + nt(lo, w)

    key_in = back(tn(sgb[...], qbig[...]) * SCALE, K_T) + back(tn(pbb[...], gbig[...]), V_T)
    kv_half[0] = key_in[0:ROWS]
    kv_half[1] = key_in[ROWS : 2 * ROWS]
    h_copy = pltpu.make_async_remote_copy(
        src_ref=kv_half.at[1 - core], dst_ref=kv_other, send_sem=h_ss, recv_sem=h_rs,
        device_id=sib, device_id_type=MESH)
    h_copy.start()

    qg = jnp.zeros((ROWS, D), F32)
    for h in range(HEADS):
        rows = slice(h * ROWS, (h + 1) * ROWS)
        qg = qg + nn(sgb[rows, :], keys) * heads_f[h]
    row_in = back(qg * SCALE, Q_T)
    for t in range(4):
        qg_send[t, 0:16, :] = row_in[t * 16 : t * 16 + 16].astype(BF16)

    h_copy.wait_recv()
    kg_send[...] = (kv_half[core] + kv_other[...]).astype(BF16).reshape(4, 16, D)

    def red_of(t):
        return 4 * t + 1 + core

    def k_copy(t):
        return pltpu.make_async_remote_copy(
            src_ref=kg_send.at[t], dst_ref=kg_recv.at[chip], send_sem=k_ss.at[t], recv_sem=k_rs,
            device_id=(2 * k + core, red_of(t)), device_id_type=MESH)

    def k_mine(t):
        return jnp.logical_and(2 * k + core == p, red_of(t) == k)

    def k_start(t, c):
        mine = k_mine(t)

        @pl.when(mine)
        def _():
            pltpu.make_async_copy(kg_send.at[t], kg_recv.at[chip], k_rs).start()

        @pl.when(jnp.logical_not(mine))
        def _():
            k_copy(t).start()

        return c

    lax.fori_loop(0, 4, k_start, 0)

    for t in range(4):
        qg_send[t, 16:32, :] = att[t * 16 : t * 16 + 16].astype(BF16)

    def q_copy(t):
        return pltpu.make_async_remote_copy(
            src_ref=qg_send.at[t], dst_ref=qg_recv.at[k], send_sem=q_ss.at[t], recv_sem=q_rs,
            device_id=(p, red_of(t)), device_id_type=MESH)

    def q_start(t, c):
        mine = red_of(t) == k

        @pl.when(mine)
        def _():
            pltpu.make_async_copy(qg_send.at[t], qg_recv.at[k], q_rs).start()

        @pl.when(jnp.logical_not(mine))
        def _():
            q_copy(t).start()

        return c

    lax.fori_loop(0, 4, q_start, 0)

    wc = pwt - jnp.mean(pwt, axis=-1, keepdims=True)
    wc_hi, wc_lo = split2(wc)
    zero16 = jnp.zeros((16, 128), BF16)
    ones8 = jnp.where(lax.broadcasted_iota(jnp.int32, (16, 128), 0) < 2, 1.0, 0.0).astype(BF16)
    rhs = jnp.concatenate(
        [jnp.concatenate([wc_hi, wc_hi, wc_lo, zero16], axis=0), jnp.concatenate([zero16, zero16, zero16, ones8], axis=0)], axis=1)
    row16 = lax.broadcasted_iota(jnp.int32, (16, 128), 0)

    def grad_body(i, c):
        r16 = pl.ds(pl.multiple_of(i * 16, 16), 16)
        sg = sgp[r16, :]
        s = jnp.sum(sg * bias[r16, :], axis=0, keepdims=True) * (1.0 / CP)
        hi, lo = split2(sg)
        s_hi = s.astype(BF16).astype(F32)
        s2 = jnp.where(row16 == 0, s_hi, jnp.where(row16 == 1, s - s_hi, 0.0)).astype(BF16)
        lhs = jnp.concatenate([hi, lo, hi, s2], axis=0)
        both = tn(lhs, rhs)
        outb[i] = (invb[i] * (both[:, :128] - nrm[i] * both[:, 128:])).astype(BF16)
        return c

    def pair_out(n):
        return pltpu.make_async_copy(outb.at[pl.ds(n * 16, 16)], pgrad_hbm.at[pl.ds(n * 16, 16)], out_sem.at[n])

    for n in range(4):
        lax.fori_loop(n * 16, (n + 1) * 16, grad_body, 0, unroll=4)
        pair_out(n).start()

    is_red = lax.rem(k, 4) == 1 + core
    t_me = quarter

    def o_copy(o):
        return pltpu.make_async_remote_copy(
            src_ref=fin_send, dst_ref=fin_recv.at[t_me], send_sem=o_ss.at[o], recv_sem=o_rs,
            device_id=ka_peer(o), device_id_type=MESH)

    @pl.when(is_red)
    def _():
        pltpu.make_async_copy(qg_recv, qg_recv, q_rs).wait()
        r16 = pl.ds(pl.multiple_of(t_me * 16, 16), 16)
        qa = jnp.sum(qg_recv[...].astype(F32), axis=0)
        g16 = gate_s[r16, :]
        att16 = qa[16:32]
        gig = cot_s[r16, :] * att16 * g16 * (1.0 - g16)
        part = qa[0:16] + back(gig, G_T)
        fin_send[16:32, :] = nn((g16 * att16).astype(BF16), weight(O_T)).astype(BF16)
        pltpu.make_async_copy(kg_recv, kg_recv, k_rs).wait()
        ig = part + jnp.sum(kg_recv[...].astype(F32), axis=0)
        n16 = nsg[r16, :]
        sgr = isg[r16, 0:1] * (
            ig - jnp.mean(ig, axis=-1, keepdims=True) - n16 * jnp.mean(ig * n16, axis=-1, keepdims=True))
        fin_send[0:16, :] = sgr.astype(BF16)

        def o_start(o, c):
            o_copy(o).start()
            return c

        lax.fori_loop(1, KA, o_start, 0)
        pltpu.make_async_copy(fin_send, fin_recv.at[t_me], o_rs).start()

    pltpu.make_async_copy(fin_recv, fin_recv, o_rs).wait()
    for t in range(4):
        sgrad_ref[t * 16 : t * 16 + 16, :] = fin_recv[t, 0:16, :]
        out_ref[t * 16 : t * 16 + 16, :] = fin_recv[t, 16:32, :]

    for n in range(4):
        pair_out(n).wait()
    x_fwd.wait_send()
    @pl.when(jnp.logical_not(self_x))
    def _():
        x_copy(0).wait_send()

    def x_done(o, c):
        x_copy(o).wait_send()
        return c

    lax.fori_loop(1, 4, x_done, 0)
    for o in range(15):
        w_copy(o).wait_send()
        f_copy(o).wait_send()

    def s_done(o, c):
        s_copy(o).wait_send()
        return c

    lax.fori_loop(1, KA, s_done, 0)

    def k_done(t, c):
        @pl.when(jnp.logical_not(k_mine(t)))
        def _():
            k_copy(t).wait_send()

        return c

    lax.fori_loop(0, 4, k_done, 0)
    h_copy.wait_send()

    def q_done(t, c):
        @pl.when(red_of(t) != k)
        def _():
            q_copy(t).wait_send()

        return c

    lax.fori_loop(0, 4, q_done, 0)

    @pl.when(is_red)
    def _():
        def o_done(o, c):
            o_copy(o).wait_send()
            return c

        lax.fori_loop(1, KA, o_done, 0)


def hand_over(out_a, sgrad_a, pgrad_a, out_b, sgrad_b, pgrad_b, out_v, sgrad_v, pgrad_v, in_sem, out_sem):
    parts = [
        (pgrad_a.at[pl.ds(n * 8, 8)], pgrad_v.at[pl.ds(n * 8, 8)], pgrad_b.at[pl.ds(n * 8, 8)]) for n in range(8)
    ]
    parts = [(out_a, out_v, out_b), (sgrad_a, sgrad_v, sgrad_b)] + parts
    for n, (src, mid, _) in enumerate(parts):
        pltpu.make_async_copy(src, mid, in_sem.at[n]).start()
    for n, (src, mid, dst) in enumerate(parts):
        pltpu.make_async_copy(src, mid, in_sem.at[n]).wait()
        pltpu.make_async_copy(mid, dst, out_sem.at[n]).start()
    for n, (_, mid, dst) in enumerate(parts):
        pltpu.make_async_copy(mid, dst, out_sem.at[n]).wait()


def local(*args):
    args = args[:10] + (args[10].T,)
    vmem = pl.BlockSpec(memory_space=pltpu.VMEM)
    hbm = pl.BlockSpec(memory_space=pltpu.HBM)
    dma = pltpu.SemaphoreType.DMA
    big = (ROWS, COLS, CP)
    flat = (HEADS * ROWS, 128)
    results = pl.pallas_call(
        kernel,
        out_shape=(
            jax.ShapeDtypeStruct((ROWS, D), BF16),
            jax.ShapeDtypeStruct((ROWS, D), BF16),
            jax.ShapeDtypeStruct(big, BF16),
        ),
        in_specs=[hbm] * 11,
        out_specs=(vmem, vmem, hbm),
        scratch_shapes=[
            pltpu.VMEM(big, BF16),
            pltpu.VMEM((ROWS, D), BF16),
            pltpu.VMEM((COLS,), jnp.int32),
            pltpu.VMEM((ROWS, D), BF16),
            pltpu.VMEM((D,), BF16),
            pltpu.VMEM((HEADS, CP), BF16),
            pltpu.VMEM(big, BF16),
            pltpu.VMEM(big, F32),
            pltpu.VMEM(big, F32),
            pltpu.VMEM(flat, F32),
            pltpu.VMEM(flat, F32),
            pltpu.VMEM((4, 16, D), BF16),
            pltpu.VMEM((ROWS, D), F32),
            pltpu.VMEM((ROWS, 128), F32),
            pltpu.VMEM((2, 4, 16, D), BF16),
            pltpu.VMEM((16, 24, 128), BF16),
            pltpu.VMEM((KA, 16, 24, 128), BF16),
            pltpu.VMEM((16, D, 128), BF16),
            pltpu.VMEM((HEADS * ROWS, D), BF16),
            pltpu.VMEM((HEADS * ROWS, D), BF16),
            pltpu.VMEM((ROWS, D), F32),
            pltpu.VMEM((ROWS, D), F32),
            pltpu.VMEM(flat, F32),
            pltpu.VMEM(flat, F32),
            pltpu.VMEM(flat, BF16),
            pltpu.VMEM(flat, BF16),
            pltpu.VMEM((KA, 24, 128), F32),
            pltpu.VMEM((24, 128), F32),
            pltpu.VMEM((2, ROWS, D), F32),
            pltpu.VMEM((ROWS, D), F32),
            pltpu.VMEM((4, 16, D), BF16),
            pltpu.VMEM((PB // 2, 16, D), BF16),
            pltpu.VMEM((4, 32, D), BF16),
            pltpu.VMEM((KA, 32, D), BF16),
            pltpu.VMEM((32, D), BF16),
            pltpu.VMEM((4, 32, D), BF16),
            dma((4,)), dma((4,)), dma((5,)), dma((16,)),
            dma((4,)), dma, dma, dma,
            dma((15,)), dma((15,)),
            dma((15,)), dma((15,)),
            dma((16,)), dma,
            dma, dma,
            dma((4,)), dma,
            dma((4,)), dma,
            dma((16,)), dma,
        ],
        compiler_params=pltpu.CompilerParams(
            collective_id=0, has_side_effects=True, vmem_limit_bytes=60 * 1024 * 1024),
    )(*args)
    return pl.pallas_call(
        hand_over,
        out_shape=tuple(jax.ShapeDtypeStruct(r.shape, r.dtype) for r in results),
        in_specs=[hbm] * 3,
        out_specs=(hbm,) * 3,
        scratch_shapes=[pltpu.VMEM(r.shape, r.dtype) for r in results] + [dma((10,)), dma((10,))],
        compiler_params=pltpu.CompilerParams(vmem_limit_bytes=60 * 1024 * 1024),
    )(*results)


def solution(mesh):
    in_specs = (
        P("pb", None), P("pb", "ka", None), P("ka"), P("pb", None), P("ka", None), P(),
        P("ka", None), P("ka", None), P("ka", None), P("ka", None), P(),
    )
    out_specs = (P("pb", None), P("pb", None), P("pb", "ka", None))
    return jax.shard_map(local, mesh=mesh, in_specs=in_specs, out_specs=out_specs, check_vma=False)
```

```python
import functools

import jax
import jax.numpy as jnp
from jax import lax
from jax.experimental import pallas as pl
from jax.experimental.pallas import tpu as pltpu
from jax.sharding import PartitionSpec as P

MESH = pl.DeviceIdType.MESH
F32 = jnp.float32
BF16 = jnp.bfloat16
EPS = 1e-05
PENALTY = 1000000000.0

ROWS = 64
COLS = 128
HEADS = 16
DIM = 24
D = 384
CP = 128
KA = 16
PB = 32
SCALE = DIM ** (-0.5)
K_T, Q_T, V_T, G_T, O_T = (0, 1, 2), (3, 4, 5), (8, 9, 10), (11, 12, 13), (6, 7, 14)
NEAR = [(a, b) for a in range(4) for b in ((0, 1, -1, 2) if a % 2 == 0 else (0, 1, -1, -2)) if (a, b) != (0, 0)]
NEAR.sort(key=lambda o: min(o[0], 4 - o[0]) + abs(o[1]))


def nt(a, b):
    return lax.dot_general(a, b, (((1,), (1,)), ((), ())), preferred_element_type=F32)


def tn(a, b):
    return lax.dot_general(a, b, (((0,), (0,)), ((), ())), preferred_element_type=F32)


def nn(a, b):
    return jnp.dot(a, b, preferred_element_type=F32)


def split2(v):
    hi = v.astype(BF16)
    return hi, (v - hi.astype(F32)).astype(BF16)


def kernel(
    single_hbm, pair_hbm, mask_hbm, ocot_hbm, wq_hbm, qb_hbm, wk_hbm, wv_hbm, wg_hbm, wo_hbm, pw_hbm,
    out_hbm, sgrad_hbm, pgrad_hbm,
    outb,    single_ref, mask_ref, ocot_ref, qb_ref, pw_ref, xp, nrm, invb, bias, sgp, a_i, nsg, isg, xall, wsend, wall, wfull, qbig, gbig, gate_s, cot_s,
    ebuf, dpbuf, sgb, pbb, stats, stat_send, kv_half, kv_other, kg_send, kg_recv, qg_send, qg_recv, fin_send,
    in_sem, out_sem, small_sem, wl_sem, x_ss, x_rs, xf_ss, xf_rs, w_ss, w_rs, f_ss, f_rs, s_ss, s_rs, h_ss, h_rs, k_ss, k_rs, q_ss, q_rs, a_ss, a_rs, o_ss, o_rs,
):
    p = lax.axis_index("pb")
    k = lax.axis_index("ka")
    core = lax.rem(p, 2)
    y = lax.rem(lax.div(p, 2), 8)
    x = lax.div(k, 4)
    z = lax.div(p, 16) * 4 + lax.rem(k, 4)
    sib = (p + 1 - 2 * core, k)
    own = lax.div(p, 2)
    quarter = lax.div(k, 4)
    rgroup = lax.rem(k, 4)
    chip = lax.div(p, 2)

    def at(x2, z2):
        x2 = lax.rem(x2 + 4, 4)
        z2 = lax.rem(z2 + 8, 8)
        return ((lax.div(z2, 4) * 8 + y) * 2 + core, x2 * 4 + lax.rem(z2, 4))

    def ka_peer(o):
        return (p, lax.rem(k + o, KA))

    def x_target(o):
        return (lax.rem(chip + o, 16) * 2 + core, own)

    def x_source(o):
        return (2 * k + core, quarter * 4 + o)

    def pair_in(n):
        return pltpu.make_async_copy(pair_hbm.at[pl.ds(n * 16, 16)], xp.at[pl.ds(n * 16, 16)], in_sem.at[n])


    bar = pltpu.get_barrier_semaphore()

    def greet_x(o, c):
        src = x_source(o)

        @pl.when(jnp.logical_or(src[0] != p, src[1] != k))
        def _():
            pl.semaphore_signal(bar, inc=1, device_id=src, device_id_type=MESH)

        return c

    lax.fori_loop(0, 4, greet_x, 0)

    def greet_ka(o, c):
        pl.semaphore_signal(bar, inc=1, device_id=ka_peer(o), device_id_type=MESH)
        return c

    lax.fori_loop(1, KA, greet_ka, 0)
    for a, b in NEAR:
        pl.semaphore_signal(bar, inc=1, device_id=at(x - a, z - b), device_id_type=MESH)
    pl.semaphore_signal(bar, inc=1, device_id=sib, device_id_type=MESH)

    single_in = pltpu.make_async_copy(single_hbm, single_ref, small_sem.at[0])
    single_in.start()
    weights_in = [
        pltpu.make_async_copy(ref.at[:, pl.ds(n * 128, 128)], wsend.at[t], wl_sem.at[t])
        for ref, tiles in ((wk_hbm, K_T), (wq_hbm, Q_T), (wv_hbm, V_T), (wg_hbm, G_T), (wo_hbm, O_T))
        for n, t in enumerate(tiles)
    ]
    for copy in weights_in:
        copy.start()
    small_in = [
        pltpu.make_async_copy(src, dst, small_sem.at[n + 1])
        for n, (src, dst) in enumerate(((mask_hbm, mask_ref), (ocot_hbm, ocot_ref), (qb_hbm, qb_ref), (pw_hbm, pw_ref)))
    ]
    for copy in small_in:
        copy.start()
    for n in range(4):
        pair_in(n).start()
    single_in.wait()
    sv = single_ref[...].astype(F32)
    cen = sv - jnp.mean(sv, axis=-1, keepdims=True)
    inv = lax.rsqrt(jnp.mean(cen * cen, axis=-1, keepdims=True) + EPS)
    normed = cen * inv
    nsg[...] = normed
    isg[...] = jnp.broadcast_to(inv, (ROWS, 128))
    a_i[...] = normed.astype(BF16).reshape(4, 16, D)

    for copy in weights_in:
        copy.wait()
    wsend[15] = jnp.zeros((24, 128), BF16)
    wall[k] = wsend[...]

    self_x = own == k
    x_sends = lax.div(own, 4) == quarter
    pl.semaphore_wait(bar, 15 + 15 + 1 + 16 * x_sends.astype(jnp.int32) - self_x.astype(jnp.int32))

    def x_copy(o):
        return pltpu.make_async_remote_copy(
            src_ref=a_i.at[rgroup], dst_ref=xall.at[core, rgroup], send_sem=x_ss.at[o], recv_sem=x_rs,
            device_id=x_target(o), device_id_type=MESH)

    def x_self():
        return pltpu.make_async_copy(a_i.at[rgroup], xall.at[core, rgroup], x_rs)

    @pl.when(self_x)
    def _():
        x_self().start()

    @pl.when(jnp.logical_and(x_sends, jnp.logical_not(self_x)))
    def _():
        x_copy(0).start()

    @pl.when(x_sends)
    def _():
        def x_send(o, c):
            x_copy(o).start()
            return c

        lax.fori_loop(1, 16, x_send, 0)

    half = pl.ds(core * 8, 8)

    def w_copy(o):
        a, b = NEAR[o]
        return pltpu.make_async_remote_copy(
            src_ref=wsend.at[half], dst_ref=wall.at[k, half], send_sem=w_ss.at[o], recv_sem=w_rs.at[o],
            device_id=at(x + a, z + b), device_id_type=MESH)

    for o in range(15):
        w_copy(o).start()

    for copy in small_in:
        copy.wait()
    pwt_b = pw_ref[...]
    pwt = pwt_b.astype(F32)

    mean_w = jnp.full((CP, CP), 1.0 / CP, BF16)

    def pair_body(n, c):
        i8 = pl.ds(pl.multiple_of(n * 8, 8), 8)
        vb = xp[i8].reshape(8 * COLS, CP)
        v = vb.astype(F32)
        cv = v - nn(vb, mean_w)
        sq_hi, sq_lo = split2(cv * cv)
        iv = lax.rsqrt(nn(sq_hi, mean_w) + nn(sq_lo, mean_w) + EPS)
        nv = cv * iv
        nrm[i8] = nv.reshape(8, COLS, CP)
        invb[i8] = iv.reshape(8, COLS, CP)
        hi, mid = split2(nv)
        both = nt(pwt_b, hi) + nt(pwt_b, mid)
        for m in range(8):
            bias[pl.ds(pl.multiple_of(n * 128 + m * 16, 16), 16), :] = both[:, m * 128 : (m + 1) * 128]
        return c

    for n in range(4):
        pair_in(n).wait()
        lax.fori_loop(n * 2, n * 2 + 2, pair_body, 0)

    def f_copy(o):
        a, b = NEAR[o]
        src = at(x - a, z - b)[1]
        return pltpu.make_async_remote_copy(
            src_ref=wall.at[src, half], dst_ref=wall.at[src, half], send_sem=f_ss.at[o], recv_sem=f_rs.at[o],
            device_id=sib, device_id_type=MESH)

    for o in range(15):
        w_copy(o).wait_recv()
        f_copy(o).start()

    pltpu.make_async_copy(xall.at[core], xall.at[core], x_rs).wait()
    x_fwd = pltpu.make_async_remote_copy(
        src_ref=xall.at[core], dst_ref=xall.at[core], send_sem=xf_ss, recv_sem=xf_rs,
        device_id=sib, device_id_type=MESH)
    x_fwd.start()

    def build(first):
        for n in range(8):
            wfull[first + n] = wall[:, first + n].astype(F32).reshape(D, 128).astype(BF16)

    build(core * 8)
    for o in range(15):
        f_copy(o).wait_recv()
    build(8 - core * 8)
    x_fwd.wait_recv()

    def weight(tiles):
        return jnp.concatenate([wfull[t] for t in tiles], axis=1)

    keys_in = xall[...].reshape(COLS, D)
    rows_in = a_i[...].reshape(ROWS, D)
    keys = nn(keys_in, weight(K_T)).astype(BF16)
    values = nn(keys_in, weight(V_T)).astype(BF16)
    queries = (nn(rows_in, weight(Q_T)) + qb_ref[...].astype(F32).reshape(1, D)).astype(BF16)
    gate = jax.nn.sigmoid(nn(rows_in, weight(G_T)))
    cot = nt(ocot_ref[...], weight(O_T))
    gate_s[...] = gate
    cot_s[...] = cot
    agrad = (gate * cot).astype(BF16)

    lane_head = lax.div(lax.broadcasted_iota(jnp.int32, (1, D), 1), DIM)
    heads_f = [jnp.where(lane_head == h, 1.0, 0.0).astype(F32) for h in range(HEADS)]
    for h in range(HEADS):
        mask_b = heads_f[h].astype(BF16)
        qbig[h * ROWS : (h + 1) * ROWS, :] = queries * mask_b
        gbig[h * ROWS : (h + 1) * ROWS, :] = agrad * mask_b

    pen = (mask_ref[...].astype(F32).reshape(1, COLS) - 1.0) * PENALTY
    lane = lax.broadcasted_iota(jnp.int32, (8, 128), 1)
    pm = jnp.zeros((8, 128), F32)
    pt = jnp.zeros((8, 128), F32)
    pd = jnp.zeros((8, 128), F32)
    for h in range(HEADS):
        rows = slice(h * ROWS, (h + 1) * ROWS)
        logits = nt(qbig[rows, :], keys) * SCALE + bias[pl.ds(h, ROWS, stride=HEADS), :] + pen
        dp = nt(gbig[rows, :], values)
        mx = jnp.max(logits, axis=-1, keepdims=True)
        e = jnp.exp(logits - mx)
        ebuf[rows, :] = e
        dpbuf[rows, :] = dp
        tot = jnp.sum(e, axis=-1, keepdims=True)
        dd = jnp.sum(e * dp, axis=-1, keepdims=True)
        for g in range(8):
            here = lane == g * 16 + h
            s8 = slice(g * 8, g * 8 + 8)
            pm = jnp.where(here, mx[s8], pm)
            pt = jnp.where(here, tot[s8], pt)
            pd = jnp.where(here, dd[s8], pd)
    stat_send[0:8, :] = pm
    stat_send[8:16, :] = pt
    stat_send[16:24, :] = pd

    def s_copy(o):
        return pltpu.make_async_remote_copy(
            src_ref=stat_send, dst_ref=stats.at[k], send_sem=s_ss.at[o], recv_sem=s_rs,
            device_id=ka_peer(o), device_id_type=MESH)

    def s_start(o, c):
        s_copy(o).start()
        return c

    lax.fori_loop(1, KA, s_start, 0)
    pltpu.make_async_copy(stat_send, stats.at[k], s_rs).start()
    num = jnp.zeros((ROWS, D), F32)
    for h in range(HEADS):
        rows = slice(h * ROWS, (h + 1) * ROWS)
        num = num + nn(ebuf[rows, :].astype(BF16), values) * heads_f[h]
    pltpu.make_async_copy(stats, stats, s_rs).wait()

    st = stats[...]
    all_m, all_t, all_d = st[:, 0:8], st[:, 8:16], st[:, 16:24]
    gm = jnp.max(all_m, axis=0)
    wts = jnp.exp(all_m - gm[None])
    gt = jnp.sum(wts * all_t, axis=0)
    gd = jnp.sum(wts * all_d, axis=0)
    coef = jnp.exp(pm - gm) / gt
    delta = gd / gt
    coef_f = jnp.zeros((ROWS, D), F32)

    for h in range(HEADS):
        rows = slice(h * ROWS, (h + 1) * ROWS)
        cc = jnp.concatenate([jnp.broadcast_to(coef[:, g * 16 + h : g * 16 + h + 1], (8, 128)) for g in range(8)], axis=0)
        dc = jnp.concatenate([jnp.broadcast_to(delta[:, g * 16 + h : g * 16 + h + 1], (8, 128)) for g in range(8)], axis=0)
        coef_f = coef_f + jnp.concatenate([cc] * 3, axis=1) * heads_f[h]
        prob = ebuf[rows, :] * cc
        sg = prob * (dpbuf[rows, :] - dc)
        sgp[pl.ds(h, ROWS, stride=HEADS), :] = sg
        sgb[rows, :] = sg.astype(BF16)
        pbb[rows, :] = prob.astype(BF16)

    att = num * coef_f

    def back(v, n):
        hi, lo = split2(v)
        w = weight(n)
        return nt(hi, w) + nt(lo, w)

    key_in = back(tn(sgb[...], qbig[...]) * SCALE, K_T) + back(tn(pbb[...], gbig[...]), V_T)
    kv_half[0] = key_in[0:ROWS]
    kv_half[1] = key_in[ROWS : 2 * ROWS]
    h_copy = pltpu.make_async_remote_copy(
        src_ref=kv_half.at[1 - core], dst_ref=kv_other, send_sem=h_ss, recv_sem=h_rs,
        device_id=sib, device_id_type=MESH)
    h_copy.start()

    qg = jnp.zeros((ROWS, D), F32)
    for h in range(HEADS):
        rows = slice(h * ROWS, (h + 1) * ROWS)
        qg = qg + nn(sgb[rows, :], keys) * heads_f[h]
    row_in = back(qg * SCALE, Q_T)
    for t in range(4):
        qg_send[t, 0:16, :] = row_in[t * 16 : t * 16 + 16].astype(BF16)

    h_copy.wait_recv()
    kg_send[...] = (kv_half[core] + kv_other[...]).astype(BF16).reshape(4, 16, D)

    def red_of(t):
        return 4 * t + 1 + core

    def k_copy(t):
        return pltpu.make_async_remote_copy(
            src_ref=kg_send.at[t], dst_ref=kg_recv.at[chip], send_sem=k_ss.at[t], recv_sem=k_rs,
            device_id=(2 * k + core, red_of(t)), device_id_type=MESH)

    def k_mine(t):
        return jnp.logical_and(2 * k + core == p, red_of(t) == k)

    def k_start(t, c):
        mine = k_mine(t)

        @pl.when(mine)
        def _():
            pltpu.make_async_copy(kg_send.at[t], kg_recv.at[chip], k_rs).start()

        @pl.when(jnp.logical_not(mine))
        def _():
            k_copy(t).start()

        return c

    lax.fori_loop(0, 4, k_start, 0)

    for t in range(4):
        qg_send[t, 16:32, :] = att[t * 16 : t * 16 + 16].astype(BF16)

    def q_copy(t):
        return pltpu.make_async_remote_copy(
            src_ref=qg_send.at[t], dst_ref=qg_recv.at[k], send_sem=q_ss.at[t], recv_sem=q_rs,
            device_id=(p, red_of(t)), device_id_type=MESH)

    def q_start(t, c):
        mine = red_of(t) == k

        @pl.when(mine)
        def _():
            pltpu.make_async_copy(qg_send.at[t], qg_recv.at[k], q_rs).start()

        @pl.when(jnp.logical_not(mine))
        def _():
            q_copy(t).start()

        return c

    lax.fori_loop(0, 4, q_start, 0)

    wc = pwt - jnp.mean(pwt, axis=-1, keepdims=True)
    wc_hi, wc_lo = split2(wc)
    zero16 = jnp.zeros((16, 128), BF16)
    ones8 = jnp.where(lax.broadcasted_iota(jnp.int32, (16, 128), 0) < 2, 1.0, 0.0).astype(BF16)
    rhs = jnp.concatenate(
        [jnp.concatenate([wc_hi, wc_hi, wc_lo, zero16], axis=0), jnp.concatenate([zero16, zero16, zero16, ones8], axis=0)], axis=1)
    row16 = lax.broadcasted_iota(jnp.int32, (16, 128), 0)

    def grad_body(i, c):
        r16 = pl.ds(pl.multiple_of(i * 16, 16), 16)
        sg = sgp[r16, :]
        s = jnp.sum(sg * bias[r16, :], axis=0, keepdims=True) * (1.0 / CP)
        hi, lo = split2(sg)
        s_hi = s.astype(BF16).astype(F32)
        s2 = jnp.where(row16 == 0, s_hi, jnp.where(row16 == 1, s - s_hi, 0.0)).astype(BF16)
        lhs = jnp.concatenate([hi, lo, hi, s2], axis=0)
        both = tn(lhs, rhs)
        outb[i] = (invb[i] * (both[:, :128] - nrm[i] * both[:, 128:])).astype(BF16)
        return c

    def pair_out(n):
        return pltpu.make_async_copy(outb.at[pl.ds(n * 16, 16)], pgrad_hbm.at[pl.ds(n * 16, 16)], out_sem.at[n])

    for n in range(4):
        lax.fori_loop(n * 16, (n + 1) * 16, grad_body, 0, unroll=4)
        pair_out(n).start()

    x_fwd.wait_send()

    @pl.when(jnp.logical_and(x_sends, jnp.logical_not(self_x)))
    def _():
        x_copy(0).wait_send()

    @pl.when(x_sends)
    def _():
        def x_done(o, c):
            x_copy(o).wait_send()
            return c

        lax.fori_loop(1, 16, x_done, 0)

    for o in range(15):
        w_copy(o).wait_send()
        f_copy(o).wait_send()

    def s_done(o, c):
        s_copy(o).wait_send()
        return c

    lax.fori_loop(1, KA, s_done, 0)

    is_red = lax.rem(k, 4) == 1 + core
    t_me = quarter

    r16 = pl.ds(pl.multiple_of(t_me * 16, 16), 16)

    def a_copy(o):
        return pltpu.make_async_remote_copy(
            src_ref=fin_send.at[0], dst_ref=out_hbm.at[r16], send_sem=a_ss.at[o], recv_sem=a_rs,
            device_id=ka_peer(o), device_id_type=MESH)

    def o_copy(o):
        return pltpu.make_async_remote_copy(
            src_ref=fin_send.at[1], dst_ref=sgrad_hbm.at[r16], send_sem=o_ss.at[o], recv_sem=o_rs,
            device_id=ka_peer(o), device_id_type=MESH)

    @pl.when(is_red)
    def _():
        pltpu.make_async_copy(qg_recv, qg_recv, q_rs).wait()
        qa = jnp.sum(qg_recv[...].astype(F32), axis=0)
        g16 = gate_s[r16, :]
        att16 = qa[16:32]
        fin_send[0] = nn((g16 * att16).astype(BF16), weight(O_T)).astype(BF16)

        def a_start(o, c):
            a_copy(o).start()
            return c

        lax.fori_loop(1, KA, a_start, 0)
        pltpu.make_async_copy(fin_send.at[0], out_hbm.at[r16], a_rs).start()
        gig = cot_s[r16, :] * att16 * g16 * (1.0 - g16)
        part = qa[0:16] + back(gig, G_T)
        pltpu.make_async_copy(kg_recv, kg_recv, k_rs).wait()
        ig = part + jnp.sum(kg_recv[...].astype(F32), axis=0)
        n16 = nsg[r16, :]
        sgr = isg[r16, 0:1] * (
            ig - jnp.mean(ig, axis=-1, keepdims=True) - n16 * jnp.mean(ig * n16, axis=-1, keepdims=True))
        fin_send[1] = sgr.astype(BF16)

        def o_start(o, c):
            o_copy(o).start()
            return c

        lax.fori_loop(1, KA, o_start, 0)
        pltpu.make_async_copy(fin_send.at[1], sgrad_hbm.at[r16], o_rs).start()

    for n in range(4):
        pair_out(n).wait()

    def k_done(t, c):
        @pl.when(jnp.logical_not(k_mine(t)))
        def _():
            k_copy(t).wait_send()

        return c

    lax.fori_loop(0, 4, k_done, 0)
    h_copy.wait_send()

    def q_done(t, c):
        @pl.when(red_of(t) != k)
        def _():
            q_copy(t).wait_send()

        return c

    lax.fori_loop(0, 4, q_done, 0)

    @pl.when(is_red)
    def _():
        def o_done(o, c):
            a_copy(o).wait_send()
            o_copy(o).wait_send()
            return c

        lax.fori_loop(1, KA, o_done, 0)

    pltpu.make_async_copy(out_hbm, out_hbm, a_rs).wait()
    pltpu.make_async_copy(sgrad_hbm, sgrad_hbm, o_rs).wait()


def hand_over(out_a, sgrad_a, pgrad_a, out_b, sgrad_b, pgrad_b, out_v, sgrad_v, pgrad_v, in_sem, out_sem):
    parts = [
        (pgrad_a.at[pl.ds(n * 8, 8)], pgrad_v.at[pl.ds(n * 8, 8)], pgrad_b.at[pl.ds(n * 8, 8)]) for n in range(8)
    ]
    parts = [(out_a, out_v, out_b), (sgrad_a, sgrad_v, sgrad_b)] + parts
    for n, (src, mid, _) in enumerate(parts):
        pltpu.make_async_copy(src, mid, in_sem.at[n]).start()
    for n, (src, mid, dst) in enumerate(parts):
        pltpu.make_async_copy(src, mid, in_sem.at[n]).wait()
        pltpu.make_async_copy(mid, dst, out_sem.at[n]).start()
    for n, (_, mid, dst) in enumerate(parts):
        pltpu.make_async_copy(mid, dst, out_sem.at[n]).wait()


def local(*args):
    args = args[:10] + (args[10].T,)
    hbm = pl.BlockSpec(memory_space=pltpu.HBM)
    dma = pltpu.SemaphoreType.DMA
    big = (ROWS, COLS, CP)
    flat = (HEADS * ROWS, 128)
    results = pl.pallas_call(
        kernel,
        out_shape=(
            jax.ShapeDtypeStruct((ROWS, D), BF16),
            jax.ShapeDtypeStruct((ROWS, D), BF16),
            jax.ShapeDtypeStruct(big, BF16),
        ),
        in_specs=[hbm] * 11,
        out_specs=(hbm, hbm, hbm),
        scratch_shapes=[
            pltpu.VMEM(big, BF16),
            pltpu.VMEM((ROWS, D), BF16),
            pltpu.VMEM((COLS,), jnp.int32),
            pltpu.VMEM((ROWS, D), BF16),
            pltpu.VMEM((D,), BF16),
            pltpu.VMEM((HEADS, CP), BF16),
            pltpu.VMEM(big, BF16),
            pltpu.VMEM(big, F32),
            pltpu.VMEM(big, F32),
            pltpu.VMEM(flat, F32),
            pltpu.VMEM(flat, F32),
            pltpu.VMEM((4, 16, D), BF16),
            pltpu.VMEM((ROWS, D), F32),
            pltpu.VMEM((ROWS, 128), F32),
            pltpu.VMEM((2, 4, 16, D), BF16),
            pltpu.VMEM((16, 24, 128), BF16),
            pltpu.VMEM((KA, 16, 24, 128), BF16),
            pltpu.VMEM((16, D, 128), BF16),
            pltpu.VMEM((HEADS * ROWS, D), BF16),
            pltpu.VMEM((HEADS * ROWS, D), BF16),
            pltpu.VMEM((ROWS, D), F32),
            pltpu.VMEM((ROWS, D), F32),
            pltpu.VMEM(flat, F32),
            pltpu.VMEM(flat, F32),
            pltpu.VMEM(flat, BF16),
            pltpu.VMEM(flat, BF16),
            pltpu.VMEM((KA, 24, 128), F32),
            pltpu.VMEM((24, 128), F32),
            pltpu.VMEM((2, ROWS, D), F32),
            pltpu.VMEM((ROWS, D), F32),
            pltpu.VMEM((4, 16, D), BF16),
            pltpu.VMEM((PB // 2, 16, D), BF16),
            pltpu.VMEM((4, 32, D), BF16),
            pltpu.VMEM((KA, 32, D), BF16),
            pltpu.VMEM((2, 16, D), BF16),
            dma((4,)), dma((4,)), dma((5,)), dma((16,)),
            dma((16,)), dma, dma, dma,
            dma((15,)), dma((15,)),
            dma((15,)), dma((15,)),
            dma((16,)), dma,
            dma, dma,
            dma((4,)), dma,
            dma((4,)), dma,
            dma((16,)), dma,
            dma((16,)), dma,
        ],
        compiler_params=pltpu.CompilerParams(
            collective_id=0, has_side_effects=True, vmem_limit_bytes=60 * 1024 * 1024),
    )(*args)
    return pl.pallas_call(
        hand_over,
        out_shape=tuple(jax.ShapeDtypeStruct(r.shape, r.dtype) for r in results),
        in_specs=[hbm] * 3,
        out_specs=(hbm,) * 3,
        scratch_shapes=[pltpu.VMEM(r.shape, r.dtype) for r in results] + [dma((10,)), dma((10,))],
        compiler_params=pltpu.CompilerParams(vmem_limit_bytes=60 * 1024 * 1024),
    )(*results)


def solution(mesh):
    in_specs = (
        P("pb", None), P("pb", "ka", None), P("ka"), P("pb", None), P("ka", None), P(),
        P("ka", None), P("ka", None), P("ka", None), P("ka", None), P(),
    )
    out_specs = (P("pb", None), P("pb", None), P("pb", "ka", None))
    return jax.shard_map(local, mesh=mesh, in_specs=in_specs, out_specs=out_specs, check_vma=False)
```

```python
import functools

import jax
import jax.numpy as jnp
from jax import lax
from jax.experimental import pallas as pl
from jax.experimental.pallas import tpu as pltpu
from jax.sharding import PartitionSpec as P

MESH = pl.DeviceIdType.MESH
F32 = jnp.float32
BF16 = jnp.bfloat16
EPS = 1e-05
PENALTY = 1000000000.0

ROWS = 64
COLS = 128
HEADS = 16
DIM = 24
D = 384
CP = 128
KA = 16
PB = 32
SCALE = DIM ** (-0.5)
K_T, Q_T, V_T, G_T, O_T = (0, 1, 2), (3, 4, 5), (8, 9, 10), (11, 12, 13), (6, 7, 14)
NEAR = [(a, b) for a in range(4) for b in ((0, 1, -1, 2) if a % 2 == 0 else (0, 1, -1, -2)) if (a, b) != (0, 0)]
NEAR.sort(key=lambda o: min(o[0], 4 - o[0]) + abs(o[1]))


def nt(a, b):
    return lax.dot_general(a, b, (((1,), (1,)), ((), ())), preferred_element_type=F32)


def tn(a, b):
    return lax.dot_general(a, b, (((0,), (0,)), ((), ())), preferred_element_type=F32)


def nn(a, b):
    return jnp.dot(a, b, preferred_element_type=F32)


def split2(v):
    hi = v.astype(BF16)
    return hi, (v - hi.astype(F32)).astype(BF16)


def kernel(
    single_hbm, pair_hbm, mask_hbm, ocot_hbm, wq_hbm, qb_hbm, wk_hbm, wv_hbm, wg_hbm, wo_hbm, pw_hbm,
    out_hbm, sgrad_hbm, pgrad_hbm,
    outb,    single_ref, mask_ref, ocot_ref, qb_ref, pw_ref, xp, nrm, invb, bias, sgp, a_i, nsg, isg, xall, wsend, wall, wfull, qbig, gbig, gate_s, cot_s, cot_send, cot_recv,
    ebuf, dpbuf, sgb, pbb, stats, stat_send, kv_half, kv_other, kg_send, kg_recv, att_send, att_recv, qg_send, qg_recv, fin_send,
    in_sem, out_sem, small_sem, wl_sem, x_ss, x_rs, xf_ss, xf_rs, c_ss, c_rs, w_ss, w_rs, f_ss, f_rs, w2_ss, w2_rs, f2_ss, f2_rs, s_ss, s_rs, h_ss, h_rs, k_ss, k_rs, t_ss, t_rs, q_ss, q_rs, a_ss, a_rs, o_ss, o_rs,
):
    p = lax.axis_index("pb")
    k = lax.axis_index("ka")
    core = lax.rem(p, 2)
    y = lax.rem(lax.div(p, 2), 8)
    x = lax.div(k, 4)
    z = lax.div(p, 16) * 4 + lax.rem(k, 4)
    sib = (p + 1 - 2 * core, k)
    own = lax.div(p, 2)
    quarter = lax.div(k, 4)
    rgroup = lax.rem(k, 4)
    chip = lax.div(p, 2)

    def at(x2, z2):
        x2 = lax.rem(x2 + 4, 4)
        z2 = lax.rem(z2 + 8, 8)
        return ((lax.div(z2, 4) * 8 + y) * 2 + core, x2 * 4 + lax.rem(z2, 4))

    def ka_peer(o):
        return (p, lax.rem(k + o, KA))

    def x_target(o):
        return (lax.rem(chip + o, 16) * 2 + core, own)

    def x_source(o):
        return (2 * k + core, quarter * 4 + o)

    def pair_in(n):
        return pltpu.make_async_copy(pair_hbm.at[pl.ds(n * 16, 16)], xp.at[pl.ds(n * 16, 16)], in_sem.at[n])


    bar = pltpu.get_barrier_semaphore()

    def greet_x(o, c):
        src = x_source(o)

        @pl.when(jnp.logical_or(src[0] != p, src[1] != k))
        def _():
            pl.semaphore_signal(bar, inc=1, device_id=src, device_id_type=MESH)

        return c

    lax.fori_loop(0, 4, greet_x, 0)

    def greet_ka(o, c):
        pl.semaphore_signal(bar, inc=1, device_id=ka_peer(o), device_id_type=MESH)
        return c

    lax.fori_loop(1, KA, greet_ka, 0)
    for a, b in NEAR:
        pl.semaphore_signal(bar, inc=1, device_id=at(x - a, z - b), device_id_type=MESH)
    pl.semaphore_signal(bar, inc=1, device_id=sib, device_id_type=MESH)

    single_in = pltpu.make_async_copy(single_hbm, single_ref, small_sem.at[0])
    single_in.start()
    weights_in = [
        pltpu.make_async_copy(ref.at[:, pl.ds(n * 128, 128)], wsend.at[t], wl_sem.at[t])
        for ref, tiles in ((wk_hbm, K_T), (wq_hbm, Q_T), (wv_hbm, V_T), (wg_hbm, G_T), (wo_hbm, O_T))
        for n, t in enumerate(tiles)
    ]
    for copy in weights_in:
        copy.start()
    small_in = [
        pltpu.make_async_copy(src, dst, small_sem.at[n + 1])
        for n, (src, dst) in enumerate(((mask_hbm, mask_ref), (ocot_hbm, ocot_ref), (qb_hbm, qb_ref), (pw_hbm, pw_ref)))
    ]
    for copy in small_in:
        copy.start()
    for n in range(4):
        pair_in(n).start()
    single_in.wait()
    sv = single_ref[...].astype(F32)
    cen = sv - jnp.mean(sv, axis=-1, keepdims=True)
    inv = lax.rsqrt(jnp.mean(cen * cen, axis=-1, keepdims=True) + EPS)
    normed = cen * inv
    nsg[...] = normed
    isg[...] = jnp.broadcast_to(inv, (ROWS, 128))
    a_i[...] = normed.astype(BF16).reshape(4, 16, D)

    for copy in weights_in:
        copy.wait()
    wsend[15] = jnp.zeros((24, 128), BF16)
    wall[k] = wsend[...]
    for copy in small_in:
        copy.wait()
    own_out = jnp.concatenate([wsend[t] for t in O_T], axis=1)
    cot_t = nt(own_out, ocot_ref[...])
    cot_send[...] = jnp.concatenate([cot_t, jnp.zeros((DIM, 128 - ROWS), F32)], axis=1).astype(BF16)

    self_x = own == k
    x_sends = lax.div(own, 4) == quarter
    pl.semaphore_wait(bar, 15 + 15 + 1 + 16 * x_sends.astype(jnp.int32) - self_x.astype(jnp.int32))

    def x_copy(o):
        return pltpu.make_async_remote_copy(
            src_ref=a_i.at[rgroup], dst_ref=xall.at[core, rgroup], send_sem=x_ss.at[o], recv_sem=x_rs,
            device_id=x_target(o), device_id_type=MESH)

    def x_self():
        return pltpu.make_async_copy(a_i.at[rgroup], xall.at[core, rgroup], x_rs)

    @pl.when(self_x)
    def _():
        x_self().start()

    @pl.when(jnp.logical_and(x_sends, jnp.logical_not(self_x)))
    def _():
        x_copy(0).start()

    @pl.when(x_sends)
    def _():
        def x_send(o, c):
            x_copy(o).start()
            return c

        lax.fori_loop(1, 16, x_send, 0)

    half = pl.ds(core * 8, 6)
    rest = pl.ds(core * 8 + 6, 2)

    def w_copy(o):
        a, b = NEAR[o]
        return pltpu.make_async_remote_copy(
            src_ref=wsend.at[half], dst_ref=wall.at[k, half], send_sem=w_ss.at[o], recv_sem=w_rs.at[o],
            device_id=at(x + a, z + b), device_id_type=MESH)

    def w2_copy(o):
        a, b = NEAR[o]
        return pltpu.make_async_remote_copy(
            src_ref=wsend.at[rest], dst_ref=wall.at[k, rest], send_sem=w2_ss.at[o], recv_sem=w2_rs.at[o],
            device_id=at(x + a, z + b), device_id_type=MESH)

    def c_copy(o):
        return pltpu.make_async_remote_copy(
            src_ref=cot_send, dst_ref=cot_recv.at[k], send_sem=c_ss.at[o], recv_sem=c_rs,
            device_id=ka_peer(o), device_id_type=MESH)

    def c_start(o, c):
        c_copy(o).start()
        return c

    lax.fori_loop(1, KA, c_start, 0)
    pltpu.make_async_copy(cot_send, cot_recv.at[k], c_rs).start()
    for o in range(15):
        w_copy(o).start()
    for o in range(15):
        w2_copy(o).start()

    pwt_b = pw_ref[...]
    pwt = pwt_b.astype(F32)

    mean_w = jnp.full((CP, CP), 1.0 / CP, BF16)

    def pair_body(n, c):
        i8 = pl.ds(pl.multiple_of(n * 8, 8), 8)
        vb = xp[i8].reshape(8 * COLS, CP)
        v = vb.astype(F32)
        cv = v - nn(vb, mean_w)
        sq_hi, sq_lo = split2(cv * cv)
        iv = lax.rsqrt(nn(sq_hi, mean_w) + nn(sq_lo, mean_w) + EPS)
        nv = cv * iv
        nrm[i8] = nv.reshape(8, COLS, CP)
        invb[i8] = iv.reshape(8, COLS, CP)
        hi, mid = split2(nv)
        both = nt(pwt_b, hi) + nt(pwt_b, mid)
        for m in range(8):
            bias[pl.ds(pl.multiple_of(n * 128 + m * 16, 16), 16), :] = both[:, m * 128 : (m + 1) * 128]
        return c

    for n in range(4):
        pair_in(n).wait()
        lax.fori_loop(n * 2, n * 2 + 2, pair_body, 0)

    def f_copy(o):
        a, b = NEAR[o]
        src = at(x - a, z - b)[1]
        return pltpu.make_async_remote_copy(
            src_ref=wall.at[src, half], dst_ref=wall.at[src, half], send_sem=f_ss.at[o], recv_sem=f_rs.at[o],
            device_id=sib, device_id_type=MESH)

    def f2_copy(o):
        a, b = NEAR[o]
        src = at(x - a, z - b)[1]
        return pltpu.make_async_remote_copy(
            src_ref=wall.at[src, rest], dst_ref=wall.at[src, rest], send_sem=f2_ss.at[o], recv_sem=f2_rs.at[o],
            device_id=sib, device_id_type=MESH)

    for o in range(15):
        w_copy(o).wait_recv()
        f_copy(o).start()

    pltpu.make_async_copy(xall.at[core], xall.at[core], x_rs).wait()
    x_fwd = pltpu.make_async_remote_copy(
        src_ref=xall.at[core], dst_ref=xall.at[core], send_sem=xf_ss, recv_sem=xf_rs,
        device_id=sib, device_id_type=MESH)
    x_fwd.start()

    def build(first, count):
        for n in range(count):
            wfull[first + n] = wall[:, first + n].astype(F32).reshape(D, 128).astype(BF16)

    build(core * 8, 6)
    for o in range(15):
        f_copy(o).wait_recv()
    build(8 - core * 8, 6)
    x_fwd.wait_recv()

    def weight(tiles):
        return jnp.concatenate([wfull[t] for t in tiles], axis=1)

    keys_in = xall[...].reshape(COLS, D)
    rows_in = a_i[...].reshape(ROWS, D)
    keys = nn(keys_in, weight(K_T)).astype(BF16)
    values = nn(keys_in, weight(V_T)).astype(BF16)
    queries = (nn(rows_in, weight(Q_T)) + qb_ref[...].astype(F32).reshape(1, D)).astype(BF16)
    gate = jax.nn.sigmoid(nn(rows_in, weight(G_T)))
    pltpu.make_async_copy(cot_recv, cot_recv, c_rs).wait()
    cot = cot_recv[...].astype(F32).reshape(D, 128).T[0:ROWS]
    gate_s[...] = gate
    cot_s[...] = cot
    agrad = (gate * cot).astype(BF16)

    lane_head = lax.div(lax.broadcasted_iota(jnp.int32, (1, D), 1), DIM)
    heads_f = [jnp.where(lane_head == h, 1.0, 0.0).astype(F32) for h in range(HEADS)]
    for h in range(HEADS):
        mask_b = heads_f[h].astype(BF16)
        qbig[h * ROWS : (h + 1) * ROWS, :] = queries * mask_b
        gbig[h * ROWS : (h + 1) * ROWS, :] = agrad * mask_b

    pen = (mask_ref[...].astype(F32).reshape(1, COLS) - 1.0) * PENALTY
    lane = lax.broadcasted_iota(jnp.int32, (8, 128), 1)
    pm = jnp.zeros((8, 128), F32)
    pt = jnp.zeros((8, 128), F32)
    pd = jnp.zeros((8, 128), F32)
    for h in range(HEADS):
        rows = slice(h * ROWS, (h + 1) * ROWS)
        logits = nt(qbig[rows, :], keys) * SCALE + bias[pl.ds(h, ROWS, stride=HEADS), :] + pen
        dp = nt(gbig[rows, :], values)
        mx = jnp.max(logits, axis=-1, keepdims=True)
        e = jnp.exp(logits - mx)
        ebuf[rows, :] = e
        dpbuf[rows, :] = dp
        tot = jnp.sum(e, axis=-1, keepdims=True)
        dd = jnp.sum(e * dp, axis=-1, keepdims=True)
        for g in range(8):
            here = lane == g * 16 + h
            s8 = slice(g * 8, g * 8 + 8)
            pm = jnp.where(here, mx[s8], pm)
            pt = jnp.where(here, tot[s8], pt)
            pd = jnp.where(here, dd[s8], pd)
    stat_send[0:8, :] = pm
    stat_send[8:16, :] = pt
    stat_send[16:24, :] = pd

    def s_copy(o):
        return pltpu.make_async_remote_copy(
            src_ref=stat_send, dst_ref=stats.at[k], send_sem=s_ss.at[o], recv_sem=s_rs,
            device_id=ka_peer(o), device_id_type=MESH)

    def s_start(o, c):
        s_copy(o).start()
        return c

    lax.fori_loop(1, KA, s_start, 0)
    pltpu.make_async_copy(stat_send, stats.at[k], s_rs).start()
    for o in range(15):
        w2_copy(o).wait_recv()
        f2_copy(o).start()
    num = jnp.zeros((ROWS, D), F32)
    for h in range(HEADS):
        rows = slice(h * ROWS, (h + 1) * ROWS)
        num = num + nn(ebuf[rows, :].astype(BF16), values) * heads_f[h]
    pltpu.make_async_copy(stats, stats, s_rs).wait()

    st = stats[...]
    all_m, all_t, all_d = st[:, 0:8], st[:, 8:16], st[:, 16:24]
    gm = jnp.max(all_m, axis=0)
    wts = jnp.exp(all_m - gm[None])
    gt = jnp.sum(wts * all_t, axis=0)
    gd = jnp.sum(wts * all_d, axis=0)
    coef = jnp.exp(pm - gm) / gt
    delta = gd / gt
    coef_f = jnp.zeros((ROWS, D), F32)
    for h in range(HEADS):
        cc = jnp.concatenate([jnp.broadcast_to(coef[:, g * 16 + h : g * 16 + h + 1], (8, 128)) for g in range(8)], axis=0)
        coef_f = coef_f + jnp.concatenate([cc] * 3, axis=1) * heads_f[h]
    att_send[...] = (num * coef_f).astype(BF16).reshape(4, 16, D)

    def red_of(t):
        return 4 * t + 1 + core

    def t_copy(t):
        return pltpu.make_async_remote_copy(
            src_ref=att_send.at[t], dst_ref=att_recv.at[k], send_sem=t_ss.at[t], recv_sem=t_rs,
            device_id=(p, red_of(t)), device_id_type=MESH)

    def t_start(t, c):
        mine = red_of(t) == k

        @pl.when(mine)
        def _():
            pltpu.make_async_copy(att_send.at[t], att_recv.at[k], t_rs).start()

        @pl.when(jnp.logical_not(mine))
        def _():
            t_copy(t).start()

        return c

    lax.fori_loop(0, 4, t_start, 0)

    for h in range(HEADS):
        rows = slice(h * ROWS, (h + 1) * ROWS)
        cc = jnp.concatenate([jnp.broadcast_to(coef[:, g * 16 + h : g * 16 + h + 1], (8, 128)) for g in range(8)], axis=0)
        dc = jnp.concatenate([jnp.broadcast_to(delta[:, g * 16 + h : g * 16 + h + 1], (8, 128)) for g in range(8)], axis=0)
        prob = ebuf[rows, :] * cc
        sg = prob * (dpbuf[rows, :] - dc)
        sgp[pl.ds(h, ROWS, stride=HEADS), :] = sg
        sgb[rows, :] = sg.astype(BF16)
        pbb[rows, :] = prob.astype(BF16)

    def back(v, n):
        hi, lo = split2(v)
        w = weight(n)
        return nt(hi, w) + nt(lo, w)

    key_in = back(tn(sgb[...], qbig[...]) * SCALE, K_T) + back(tn(pbb[...], gbig[...]), V_T)
    kv_half[0] = key_in[0:ROWS]
    kv_half[1] = key_in[ROWS : 2 * ROWS]
    h_copy = pltpu.make_async_remote_copy(
        src_ref=kv_half.at[1 - core], dst_ref=kv_other, send_sem=h_ss, recv_sem=h_rs,
        device_id=sib, device_id_type=MESH)
    h_copy.start()

    qg = jnp.zeros((ROWS, D), F32)
    for h in range(HEADS):
        rows = slice(h * ROWS, (h + 1) * ROWS)
        qg = qg + nn(sgb[rows, :], keys) * heads_f[h]
    row_in = back(qg * SCALE, Q_T)
    qg_send[...] = row_in.astype(BF16).reshape(4, 16, D)

    def q_copy(t):
        return pltpu.make_async_remote_copy(
            src_ref=qg_send.at[t], dst_ref=qg_recv.at[k], send_sem=q_ss.at[t], recv_sem=q_rs,
            device_id=(p, red_of(t)), device_id_type=MESH)

    def q_start(t, c):
        mine = red_of(t) == k

        @pl.when(mine)
        def _():
            pltpu.make_async_copy(qg_send.at[t], qg_recv.at[k], q_rs).start()

        @pl.when(jnp.logical_not(mine))
        def _():
            q_copy(t).start()

        return c

    lax.fori_loop(0, 4, q_start, 0)

    h_copy.wait_recv()
    kg_send[...] = (kv_half[core] + kv_other[...]).astype(BF16).reshape(4, 16, D)

    def k_copy(t):
        return pltpu.make_async_remote_copy(
            src_ref=kg_send.at[t], dst_ref=kg_recv.at[chip], send_sem=k_ss.at[t], recv_sem=k_rs,
            device_id=(2 * k + core, red_of(t)), device_id_type=MESH)

    def k_mine(t):
        return jnp.logical_and(2 * k + core == p, red_of(t) == k)

    def k_start(t, c):
        mine = k_mine(t)

        @pl.when(mine)
        def _():
            pltpu.make_async_copy(kg_send.at[t], kg_recv.at[chip], k_rs).start()

        @pl.when(jnp.logical_not(mine))
        def _():
            k_copy(t).start()

        return c

    lax.fori_loop(0, 4, k_start, 0)

    wc = pwt - jnp.mean(pwt, axis=-1, keepdims=True)
    wc_hi, wc_lo = split2(wc)
    zero16 = jnp.zeros((16, 128), BF16)
    ones8 = jnp.where(lax.broadcasted_iota(jnp.int32, (16, 128), 0) < 2, 1.0, 0.0).astype(BF16)
    rhs = jnp.concatenate(
        [jnp.concatenate([wc_hi, wc_hi, wc_lo, zero16], axis=0), jnp.concatenate([zero16, zero16, zero16, ones8], axis=0)], axis=1)
    row16 = lax.broadcasted_iota(jnp.int32, (16, 128), 0)

    def grad_body(i, c):
        r16 = pl.ds(pl.multiple_of(i * 16, 16), 16)
        sg = sgp[r16, :]
        s = jnp.sum(sg * bias[r16, :], axis=0, keepdims=True) * (1.0 / CP)
        hi, lo = split2(sg)
        s_hi = s.astype(BF16).astype(F32)
        s2 = jnp.where(row16 == 0, s_hi, jnp.where(row16 == 1, s - s_hi, 0.0)).astype(BF16)
        lhs = jnp.concatenate([hi, lo, hi, s2], axis=0)
        both = tn(lhs, rhs)
        outb[i] = (invb[i] * (both[:, :128] - nrm[i] * both[:, 128:])).astype(BF16)
        return c

    def pair_out(n):
        return pltpu.make_async_copy(outb.at[pl.ds(n * 16, 16)], pgrad_hbm.at[pl.ds(n * 16, 16)], out_sem.at[n])

    for n in range(4):
        lax.fori_loop(n * 16, (n + 1) * 16, grad_body, 0, unroll=4)
        pair_out(n).start()

    for o in range(15):
        f2_copy(o).wait_recv()
    build(6, 2)
    build(14, 2)

    x_fwd.wait_send()

    @pl.when(jnp.logical_and(x_sends, jnp.logical_not(self_x)))
    def _():
        x_copy(0).wait_send()

    @pl.when(x_sends)
    def _():
        def x_done(o, c):
            x_copy(o).wait_send()
            return c

        lax.fori_loop(1, 16, x_done, 0)

    for o in range(15):
        w_copy(o).wait_send()
        f_copy(o).wait_send()
        w2_copy(o).wait_send()
        f2_copy(o).wait_send()

    def s_done(o, c):
        s_copy(o).wait_send()
        c_copy(o).wait_send()
        return c

    lax.fori_loop(1, KA, s_done, 0)

    is_red = lax.rem(k, 4) == 1 + core
    t_me = quarter

    r16 = pl.ds(pl.multiple_of(t_me * 16, 16), 16)

    def a_copy(o):
        return pltpu.make_async_remote_copy(
            src_ref=fin_send.at[0], dst_ref=out_hbm.at[r16], send_sem=a_ss.at[o], recv_sem=a_rs,
            device_id=ka_peer(o), device_id_type=MESH)

    def o_copy(o):
        return pltpu.make_async_remote_copy(
            src_ref=fin_send.at[1], dst_ref=sgrad_hbm.at[r16], send_sem=o_ss.at[o], recv_sem=o_rs,
            device_id=ka_peer(o), device_id_type=MESH)

    @pl.when(is_red)
    def _():
        pltpu.make_async_copy(att_recv, att_recv, t_rs).wait()
        att16 = jnp.sum(att_recv[...].astype(F32), axis=0)
        g16 = gate_s[r16, :]
        fin_send[0] = nn((g16 * att16).astype(BF16), weight(O_T)).astype(BF16)

        def a_start(o, c):
            a_copy(o).start()
            return c

        lax.fori_loop(1, KA, a_start, 0)
        pltpu.make_async_copy(fin_send.at[0], out_hbm.at[r16], a_rs).start()
        gig = cot_s[r16, :] * att16 * g16 * (1.0 - g16)
        part = back(gig, G_T)
        pltpu.make_async_copy(qg_recv, qg_recv, q_rs).wait()
        part = part + jnp.sum(qg_recv[...].astype(F32), axis=0)
        pltpu.make_async_copy(kg_recv, kg_recv, k_rs).wait()
        ig = part + jnp.sum(kg_recv[...].astype(F32), axis=0)
        n16 = nsg[r16, :]
        sgr = isg[r16, 0:1] * (
            ig - jnp.mean(ig, axis=-1, keepdims=True) - n16 * jnp.mean(ig * n16, axis=-1, keepdims=True))
        fin_send[1] = sgr.astype(BF16)

        def o_start(o, c):
            o_copy(o).start()
            return c

        lax.fori_loop(1, KA, o_start, 0)
        pltpu.make_async_copy(fin_send.at[1], sgrad_hbm.at[r16], o_rs).start()

    for n in range(4):
        pair_out(n).wait()

    def k_done(t, c):
        @pl.when(jnp.logical_not(k_mine(t)))
        def _():
            k_copy(t).wait_send()

        return c

    lax.fori_loop(0, 4, k_done, 0)
    h_copy.wait_send()

    def q_done(t, c):
        @pl.when(red_of(t) != k)
        def _():
            q_copy(t).wait_send()
            t_copy(t).wait_send()

        return c

    lax.fori_loop(0, 4, q_done, 0)

    @pl.when(is_red)
    def _():
        def o_done(o, c):
            a_copy(o).wait_send()
            o_copy(o).wait_send()
            return c

        lax.fori_loop(1, KA, o_done, 0)

    pltpu.make_async_copy(out_hbm, out_hbm, a_rs).wait()
    pltpu.make_async_copy(sgrad_hbm, sgrad_hbm, o_rs).wait()


def hand_over(out_a, sgrad_a, pgrad_a, out_b, sgrad_b, pgrad_b, out_v, sgrad_v, pgrad_v, in_sem, out_sem):
    parts = [
        (pgrad_a.at[pl.ds(n * 8, 8)], pgrad_v.at[pl.ds(n * 8, 8)], pgrad_b.at[pl.ds(n * 8, 8)]) for n in range(8)
    ]
    parts = [(out_a, out_v, out_b), (sgrad_a, sgrad_v, sgrad_b)] + parts
    for n, (src, mid, _) in enumerate(parts):
        pltpu.make_async_copy(src, mid, in_sem.at[n]).start()
    for n, (src, mid, dst) in enumerate(parts):
        pltpu.make_async_copy(src, mid, in_sem.at[n]).wait()
        pltpu.make_async_copy(mid, dst, out_sem.at[n]).start()
    for n, (_, mid, dst) in enumerate(parts):
        pltpu.make_async_copy(mid, dst, out_sem.at[n]).wait()


def local(*args):
    args = args[:10] + (args[10].T,)
    hbm = pl.BlockSpec(memory_space=pltpu.HBM)
    dma = pltpu.SemaphoreType.DMA
    big = (ROWS, COLS, CP)
    flat = (HEADS * ROWS, 128)
    results = pl.pallas_call(
        kernel,
        out_shape=(
            jax.ShapeDtypeStruct((ROWS, D), BF16),
            jax.ShapeDtypeStruct((ROWS, D), BF16),
            jax.ShapeDtypeStruct(big, BF16),
        ),
        in_specs=[hbm] * 11,
        out_specs=(hbm, hbm, hbm),
        scratch_shapes=[
            pltpu.VMEM(big, BF16),
            pltpu.VMEM((ROWS, D), BF16),
            pltpu.VMEM((COLS,), jnp.int32),
            pltpu.VMEM((ROWS, D), BF16),
            pltpu.VMEM((D,), BF16),
            pltpu.VMEM((HEADS, CP), BF16),
            pltpu.VMEM(big, BF16),
            pltpu.VMEM(big, F32),
            pltpu.VMEM(big, F32),
            pltpu.VMEM(flat, F32),
            pltpu.VMEM(flat, F32),
            pltpu.VMEM((4, 16, D), BF16),
            pltpu.VMEM((ROWS, D), F32),
            pltpu.VMEM((ROWS, 128), F32),
            pltpu.VMEM((2, 4, 16, D), BF16),
            pltpu.VMEM((16, 24, 128), BF16),
            pltpu.VMEM((KA, 16, 24, 128), BF16),
            pltpu.VMEM((16, D, 128), BF16),
            pltpu.VMEM((HEADS * ROWS, D), BF16),
            pltpu.VMEM((HEADS * ROWS, D), BF16),
            pltpu.VMEM((ROWS, D), F32),
            pltpu.VMEM((ROWS, D), F32),
            pltpu.VMEM((DIM, 128), BF16),
            pltpu.VMEM((KA, DIM, 128), BF16),
            pltpu.VMEM(flat, F32),
            pltpu.VMEM(flat, F32),
            pltpu.VMEM(flat, BF16),
            pltpu.VMEM(flat, BF16),
            pltpu.VMEM((KA, 24, 128), F32),
            pltpu.VMEM((24, 128), F32),
            pltpu.VMEM((2, ROWS, D), F32),
            pltpu.VMEM((ROWS, D), F32),
            pltpu.VMEM((4, 16, D), BF16),
            pltpu.VMEM((PB // 2, 16, D), BF16),
            pltpu.VMEM((4, 16, D), BF16),
            pltpu.VMEM((KA, 16, D), BF16),
            pltpu.VMEM((4, 16, D), BF16),
            pltpu.VMEM((KA, 16, D), BF16),
            pltpu.VMEM((2, 16, D), BF16),
            dma((4,)), dma((4,)), dma((5,)), dma((16,)),
            dma((16,)), dma, dma, dma,
            dma((16,)), dma,
            dma((15,)), dma((15,)),
            dma((15,)), dma((15,)),
            dma((15,)), dma((15,)),
            dma((15,)), dma((15,)),
            dma((16,)), dma,
            dma, dma,
            dma((4,)), dma,
            dma((4,)), dma,
            dma((4,)), dma,
            dma((16,)), dma,
            dma((16,)), dma,
        ],
        compiler_params=pltpu.CompilerParams(
            collective_id=0, has_side_effects=True, vmem_limit_bytes=60 * 1024 * 1024),
    )(*args)
    return pl.pallas_call(
        hand_over,
        out_shape=tuple(jax.ShapeDtypeStruct(r.shape, r.dtype) for r in results),
        in_specs=[hbm] * 3,
        out_specs=(hbm,) * 3,
        scratch_shapes=[pltpu.VMEM(r.shape, r.dtype) for r in results] + [dma((10,)), dma((10,))],
        compiler_params=pltpu.CompilerParams(vmem_limit_bytes=60 * 1024 * 1024),
    )(*results)


def solution(mesh):
    in_specs = (
        P("pb", None), P("pb", "ka", None), P("ka"), P("pb", None), P("ka", None), P(),
        P("ka", None), P("ka", None), P("ka", None), P("ka", None), P(),
    )
    out_specs = (P("pb", None), P("pb", None), P("pb", "ka", None))
    return jax.shard_map(local, mesh=mesh, in_specs=in_specs, out_specs=out_specs, check_vma=False)
```

```python
import functools

import jax
import jax.numpy as jnp
from jax import lax
from jax.experimental import pallas as pl
from jax.experimental.pallas import tpu as pltpu
from jax.sharding import PartitionSpec as P

MESH = pl.DeviceIdType.MESH
F32 = jnp.float32
BF16 = jnp.bfloat16
EPS = 1e-05
PENALTY = 1000000000.0

ROWS = 64
COLS = 128
HEADS = 16
DIM = 24
D = 384
CP = 128
KA = 16
PB = 32
SCALE = DIM ** (-0.5)
K_T, Q_T, V_T, G_T, O_T = (0, 1, 2), (3, 4, 5), (8, 9, 10), (11, 12, 13), (6, 7, 14)
NEAR = [(a, b) for a in range(4) for b in ((0, 1, -1, 2) if a % 2 == 0 else (0, 1, -1, -2)) if (a, b) != (0, 0)]
NEAR.sort(key=lambda o: min(o[0], 4 - o[0]) + abs(o[1]))


def nt(a, b):
    return lax.dot_general(a, b, (((1,), (1,)), ((), ())), preferred_element_type=F32)


def tn(a, b):
    return lax.dot_general(a, b, (((0,), (0,)), ((), ())), preferred_element_type=F32)


def nn(a, b):
    return jnp.dot(a, b, preferred_element_type=F32)


def split2(v):
    hi = v.astype(BF16)
    return hi, (v - hi.astype(F32)).astype(BF16)


def kernel(
    single_hbm, pair_hbm, mask_hbm, ocot_hbm, wq_hbm, qb_hbm, wk_hbm, wv_hbm, wg_hbm, wo_hbm, pw_hbm,
    out_hbm, sgrad_hbm, pgrad_hbm,
    outb,    single_ref, mask_ref, ocot_ref, qb_ref, pw_ref, xp, nrm, invb, bias, sgp, a_i, nsg, isg, xall, wsend, wall, wfull, qbig, gbig, gate_s, cot_s,
    ebuf, dpbuf, sgb, pbb, stats, stat_send, kv_half, kv_other, kg_send, kg_recv, att_send, att_recv, qg_send, qg_recv, fin_send,
    in_sem, out_sem, small_sem, wl_sem, x_ss, x_rs, xf_ss, xf_rs, w_ss, w_rs, f_ss, f_rs, s_ss, s_rs, h_ss, h_rs, k_ss, k_rs, t_ss, t_rs, q_ss, q_rs, a_ss, a_rs, o_ss, o_rs,
):
    p = lax.axis_index("pb")
    k = lax.axis_index("ka")
    core = lax.rem(p, 2)
    y = lax.rem(lax.div(p, 2), 8)
    x = lax.div(k, 4)
    z = lax.div(p, 16) * 4 + lax.rem(k, 4)
    sib = (p + 1 - 2 * core, k)
    own = lax.div(p, 2)
    quarter = lax.div(k, 4)
    rgroup = lax.rem(k, 4)
    chip = lax.div(p, 2)

    def at(x2, z2):
        x2 = lax.rem(x2 + 4, 4)
        z2 = lax.rem(z2 + 8, 8)
        return ((lax.div(z2, 4) * 8 + y) * 2 + core, x2 * 4 + lax.rem(z2, 4))

    def ka_peer(o):
        return (p, lax.rem(k + o, KA))

    def x_target(o):
        return (lax.rem(chip + o, 16) * 2 + core, own)

    def x_source(o):
        return (2 * k + core, quarter * 4 + o)

    def pair_in(n):
        return pltpu.make_async_copy(pair_hbm.at[pl.ds(n * 16, 16)], xp.at[pl.ds(n * 16, 16)], in_sem.at[n])


    bar = pltpu.get_barrier_semaphore()

    def greet_x(o, c):
        src = x_source(o)

        @pl.when(jnp.logical_or(src[0] != p, src[1] != k))
        def _():
            pl.semaphore_signal(bar, inc=1, device_id=src, device_id_type=MESH)

        return c

    lax.fori_loop(0, 4, greet_x, 0)

    def greet_ka(o, c):
        pl.semaphore_signal(bar, inc=1, device_id=ka_peer(o), device_id_type=MESH)
        return c

    lax.fori_loop(1, KA, greet_ka, 0)
    for a, b in NEAR:
        pl.semaphore_signal(bar, inc=1, device_id=at(x - a, z - b), device_id_type=MESH)
    pl.semaphore_signal(bar, inc=1, device_id=sib, device_id_type=MESH)

    single_in = pltpu.make_async_copy(single_hbm, single_ref, small_sem.at[0])
    single_in.start()
    weights_in = [
        pltpu.make_async_copy(ref.at[:, pl.ds(n * 128, 128)], wsend.at[t], wl_sem.at[t])
        for ref, tiles in ((wk_hbm, K_T), (wq_hbm, Q_T), (wv_hbm, V_T), (wg_hbm, G_T), (wo_hbm, O_T))
        for n, t in enumerate(tiles)
    ]
    for copy in weights_in:
        copy.start()
    small_in = [
        pltpu.make_async_copy(src, dst, small_sem.at[n + 1])
        for n, (src, dst) in enumerate(((mask_hbm, mask_ref), (ocot_hbm, ocot_ref), (qb_hbm, qb_ref), (pw_hbm, pw_ref)))
    ]
    for copy in small_in:
        copy.start()
    for n in range(4):
        pair_in(n).start()
    single_in.wait()
    sv = single_ref[...].astype(F32)
    cen = sv - jnp.mean(sv, axis=-1, keepdims=True)
    inv = lax.rsqrt(jnp.mean(cen * cen, axis=-1, keepdims=True) + EPS)
    normed = cen * inv
    nsg[...] = normed
    isg[...] = jnp.broadcast_to(inv, (ROWS, 128))
    a_i[...] = normed.astype(BF16).reshape(4, 16, D)

    for copy in weights_in:
        copy.wait()
    wsend[15] = jnp.zeros((24, 128), BF16)
    wall[k] = wsend[...]

    self_x = own == k
    x_sends = lax.div(own, 4) == quarter
    pl.semaphore_wait(bar, 15 + 15 + 1 + 16 * x_sends.astype(jnp.int32) - self_x.astype(jnp.int32))

    def x_copy(o):
        return pltpu.make_async_remote_copy(
            src_ref=a_i.at[rgroup], dst_ref=xall.at[core, rgroup], send_sem=x_ss.at[o], recv_sem=x_rs,
            device_id=x_target(o), device_id_type=MESH)

    def x_self():
        return pltpu.make_async_copy(a_i.at[rgroup], xall.at[core, rgroup], x_rs)

    @pl.when(self_x)
    def _():
        x_self().start()

    @pl.when(jnp.logical_and(x_sends, jnp.logical_not(self_x)))
    def _():
        x_copy(0).start()

    @pl.when(x_sends)
    def _():
        def x_send(o, c):
            x_copy(o).start()
            return c

        lax.fori_loop(1, 16, x_send, 0)

    half = pl.ds(core * 8, 8)

    def w_copy(o):
        a, b = NEAR[o]
        return pltpu.make_async_remote_copy(
            src_ref=wsend.at[half], dst_ref=wall.at[k, half], send_sem=w_ss.at[o], recv_sem=w_rs.at[o],
            device_id=at(x + a, z + b), device_id_type=MESH)

    for o in range(15):
        w_copy(o).start()

    for copy in small_in:
        copy.wait()
    pwt_b = pw_ref[...]
    pwt = pwt_b.astype(F32)

    mean_w = jnp.full((CP, CP), 1.0 / CP, BF16)

    def pair_body(n, c):
        i8 = pl.ds(pl.multiple_of(n * 8, 8), 8)
        vb = xp[i8].reshape(8 * COLS, CP)
        v = vb.astype(F32)
        cv = v - nn(vb, mean_w)
        sq_hi, sq_lo = split2(cv * cv)
        iv = lax.rsqrt(nn(sq_hi, mean_w) + nn(sq_lo, mean_w) + EPS)
        nv = cv * iv
        nrm[i8] = nv.reshape(8, COLS, CP)
        invb[i8] = iv.reshape(8, COLS, CP)
        hi, mid = split2(nv)
        both = nt(pwt_b, hi) + nt(pwt_b, mid)
        for m in range(8):
            bias[pl.ds(pl.multiple_of(n * 128 + m * 16, 16), 16), :] = both[:, m * 128 : (m + 1) * 128]
        return c

    for n in range(4):
        pair_in(n).wait()
        lax.fori_loop(n * 2, n * 2 + 2, pair_body, 0)

    def f_copy(o):
        a, b = NEAR[o]
        src = at(x - a, z - b)[1]
        return pltpu.make_async_remote_copy(
            src_ref=wall.at[src, half], dst_ref=wall.at[src, half], send_sem=f_ss.at[o], recv_sem=f_rs.at[o],
            device_id=sib, device_id_type=MESH)

    for o in range(15):
        w_copy(o).wait_recv()
        f_copy(o).start()

    pltpu.make_async_copy(xall.at[core], xall.at[core], x_rs).wait()
    x_fwd = pltpu.make_async_remote_copy(
        src_ref=xall.at[core], dst_ref=xall.at[core], send_sem=xf_ss, recv_sem=xf_rs,
        device_id=sib, device_id_type=MESH)
    x_fwd.start()

    def build(first):
        for n in range(8):
            wfull[first + n] = wall[:, first + n].astype(F32).reshape(D, 128).astype(BF16)

    build(core * 8)
    for o in range(15):
        f_copy(o).wait_recv()
    build(8 - core * 8)
    x_fwd.wait_recv()

    def weight(tiles):
        return jnp.concatenate([wfull[t] for t in tiles], axis=1)

    keys_in = xall[...].reshape(COLS, D)
    rows_in = a_i[...].reshape(ROWS, D)
    keys = nn(keys_in, weight(K_T)).astype(BF16)
    values = nn(keys_in, weight(V_T)).astype(BF16)
    queries = (nn(rows_in, weight(Q_T)) + qb_ref[...].astype(F32).reshape(1, D)).astype(BF16)
    gate = jax.nn.sigmoid(nn(rows_in, weight(G_T)))
    cot = nt(ocot_ref[...], weight(O_T))
    gate_s[...] = gate
    cot_s[...] = cot
    agrad = (gate * cot).astype(BF16)

    lane_head = lax.div(lax.broadcasted_iota(jnp.int32, (1, D), 1), DIM)
    heads_f = [jnp.where(lane_head == h, 1.0, 0.0).astype(F32) for h in range(HEADS)]
    for h in range(HEADS):
        mask_b = heads_f[h].astype(BF16)
        qbig[h * ROWS : (h + 1) * ROWS, :] = queries * mask_b
        gbig[h * ROWS : (h + 1) * ROWS, :] = agrad * mask_b

    pen = (mask_ref[...].astype(F32).reshape(1, COLS) - 1.0) * PENALTY
    lane = lax.broadcasted_iota(jnp.int32, (8, 128), 1)
    pm = jnp.zeros((8, 128), F32)
    pt = jnp.zeros((8, 128), F32)
    pd = jnp.zeros((8, 128), F32)
    for h in range(HEADS):
        rows = slice(h * ROWS, (h + 1) * ROWS)
        logits = nt(qbig[rows, :], keys) * SCALE + bias[pl.ds(h, ROWS, stride=HEADS), :] + pen
        dp = nt(gbig[rows, :], values)
        mx = jnp.max(logits, axis=-1, keepdims=True)
        e = jnp.exp(logits - mx)
        ebuf[rows, :] = e
        dpbuf[rows, :] = dp
        tot = jnp.sum(e, axis=-1, keepdims=True)
        dd = jnp.sum(e * dp, axis=-1, keepdims=True)
        for g in range(8):
            here = lane == g * 16 + h
            s8 = slice(g * 8, g * 8 + 8)
            pm = jnp.where(here, mx[s8], pm)
            pt = jnp.where(here, tot[s8], pt)
            pd = jnp.where(here, dd[s8], pd)
    stat_send[0:8, :] = pm
    stat_send[8:16, :] = pt
    stat_send[16:24, :] = pd

    def s_copy(o):
        return pltpu.make_async_remote_copy(
            src_ref=stat_send, dst_ref=stats.at[k], send_sem=s_ss.at[o], recv_sem=s_rs,
            device_id=ka_peer(o), device_id_type=MESH)

    def s_start(o, c):
        s_copy(o).start()
        return c

    lax.fori_loop(1, KA, s_start, 0)
    pltpu.make_async_copy(stat_send, stats.at[k], s_rs).start()
    num = jnp.zeros((ROWS, D), F32)
    for h in range(HEADS):
        rows = slice(h * ROWS, (h + 1) * ROWS)
        num = num + nn(ebuf[rows, :].astype(BF16), values) * heads_f[h]
    pltpu.make_async_copy(stats, stats, s_rs).wait()

    st = stats[...]
    all_m, all_t, all_d = st[:, 0:8], st[:, 8:16], st[:, 16:24]
    gm = jnp.max(all_m, axis=0)
    wts = jnp.exp(all_m - gm[None])
    gt = jnp.sum(wts * all_t, axis=0)
    gd = jnp.sum(wts * all_d, axis=0)
    coef = jnp.exp(pm - gm) / gt
    delta = gd / gt
    coef_f = jnp.zeros((ROWS, D), F32)
    for h in range(HEADS):
        cc = jnp.concatenate([jnp.broadcast_to(coef[:, g * 16 + h : g * 16 + h + 1], (8, 128)) for g in range(8)], axis=0)
        coef_f = coef_f + jnp.concatenate([cc] * 3, axis=1) * heads_f[h]
    att_send[...] = (num * coef_f).astype(BF16).reshape(4, 16, D)

    def red_of(t):
        return 4 * t + 1 + core

    def t_copy(t):
        return pltpu.make_async_remote_copy(
            src_ref=att_send.at[t], dst_ref=att_recv.at[k], send_sem=t_ss.at[t], recv_sem=t_rs,
            device_id=(p, red_of(t)), device_id_type=MESH)

    def t_start(t, c):
        mine = red_of(t) == k

        @pl.when(mine)
        def _():
            pltpu.make_async_copy(att_send.at[t], att_recv.at[k], t_rs).start()

        @pl.when(jnp.logical_not(mine))
        def _():
            t_copy(t).start()

        return c

    lax.fori_loop(0, 4, t_start, 0)

    for h in range(HEADS):
        rows = slice(h * ROWS, (h + 1) * ROWS)
        cc = jnp.concatenate([jnp.broadcast_to(coef[:, g * 16 + h : g * 16 + h + 1], (8, 128)) for g in range(8)], axis=0)
        dc = jnp.concatenate([jnp.broadcast_to(delta[:, g * 16 + h : g * 16 + h + 1], (8, 128)) for g in range(8)], axis=0)
        prob = ebuf[rows, :] * cc
        sg = prob * (dpbuf[rows, :] - dc)
        sgp[pl.ds(h, ROWS, stride=HEADS), :] = sg
        sgb[rows, :] = sg.astype(BF16)
        pbb[rows, :] = prob.astype(BF16)

    def back(v, n):
        hi, lo = split2(v)
        w = weight(n)
        return nt(hi, w) + nt(lo, w)

    key_in = nt((tn(sgb[...], qbig[...]) * SCALE).astype(BF16), weight(K_T)) + nt(
        tn(pbb[...], gbig[...]).astype(BF16), weight(V_T))
    kv_half[0] = key_in[0:ROWS]
    kv_half[1] = key_in[ROWS : 2 * ROWS]
    h_copy = pltpu.make_async_remote_copy(
        src_ref=kv_half.at[1 - core], dst_ref=kv_other, send_sem=h_ss, recv_sem=h_rs,
        device_id=sib, device_id_type=MESH)
    h_copy.start()

    qg = jnp.zeros((ROWS, D), F32)
    for h in range(HEADS):
        rows = slice(h * ROWS, (h + 1) * ROWS)
        qg = qg + nn(sgb[rows, :], keys) * heads_f[h]
    row_in = nt((qg * SCALE).astype(BF16), weight(Q_T))
    qg_send[...] = row_in.astype(BF16).reshape(4, 16, D)

    def q_copy(t):
        return pltpu.make_async_remote_copy(
            src_ref=qg_send.at[t], dst_ref=qg_recv.at[k], send_sem=q_ss.at[t], recv_sem=q_rs,
            device_id=(p, red_of(t)), device_id_type=MESH)

    def q_start(t, c):
        mine = red_of(t) == k

        @pl.when(mine)
        def _():
            pltpu.make_async_copy(qg_send.at[t], qg_recv.at[k], q_rs).start()

        @pl.when(jnp.logical_not(mine))
        def _():
            q_copy(t).start()

        return c

    lax.fori_loop(0, 4, q_start, 0)

    h_copy.wait_recv()
    kg_send[...] = (kv_half[core] + kv_other[...]).astype(BF16).reshape(4, 16, D)

    def k_copy(t):
        return pltpu.make_async_remote_copy(
            src_ref=kg_send.at[t], dst_ref=kg_recv.at[chip], send_sem=k_ss.at[t], recv_sem=k_rs,
            device_id=(2 * k + core, red_of(t)), device_id_type=MESH)

    def k_mine(t):
        return jnp.logical_and(2 * k + core == p, red_of(t) == k)

    def k_start(t, c):
        mine = k_mine(t)

        @pl.when(mine)
        def _():
            pltpu.make_async_copy(kg_send.at[t], kg_recv.at[chip], k_rs).start()

        @pl.when(jnp.logical_not(mine))
        def _():
            k_copy(t).start()

        return c

    lax.fori_loop(0, 4, k_start, 0)

    wc = pwt - jnp.mean(pwt, axis=-1, keepdims=True)
    wc_hi, wc_lo = split2(wc)
    zero16 = jnp.zeros((16, 128), BF16)
    ones8 = jnp.where(lax.broadcasted_iota(jnp.int32, (16, 128), 0) < 2, 1.0, 0.0).astype(BF16)
    rhs = jnp.concatenate(
        [jnp.concatenate([wc_hi, wc_hi, wc_lo, zero16], axis=0), jnp.concatenate([zero16, zero16, zero16, ones8], axis=0)], axis=1)
    row16 = lax.broadcasted_iota(jnp.int32, (16, 128), 0)

    def grad_body(i, c):
        r16 = pl.ds(pl.multiple_of(i * 16, 16), 16)
        sg = sgp[r16, :]
        s = jnp.sum(sg * bias[r16, :], axis=0, keepdims=True) * (1.0 / CP)
        hi, lo = split2(sg)
        s_hi = s.astype(BF16).astype(F32)
        s2 = jnp.where(row16 == 0, s_hi, jnp.where(row16 == 1, s - s_hi, 0.0)).astype(BF16)
        lhs = jnp.concatenate([hi, lo, hi, s2], axis=0)
        both = tn(lhs, rhs)
        outb[i] = (invb[i] * (both[:, :128] - nrm[i] * both[:, 128:])).astype(BF16)
        return c

    def pair_out(n):
        return pltpu.make_async_copy(outb.at[pl.ds(n * 16, 16)], pgrad_hbm.at[pl.ds(n * 16, 16)], out_sem.at[n])

    for n in range(4):
        lax.fori_loop(n * 16, (n + 1) * 16, grad_body, 0, unroll=4)
        pair_out(n).start()

    x_fwd.wait_send()

    @pl.when(jnp.logical_and(x_sends, jnp.logical_not(self_x)))
    def _():
        x_copy(0).wait_send()

    @pl.when(x_sends)
    def _():
        def x_done(o, c):
            x_copy(o).wait_send()
            return c

        lax.fori_loop(1, 16, x_done, 0)

    for o in range(15):
        w_copy(o).wait_send()
        f_copy(o).wait_send()

    def s_done(o, c):
        s_copy(o).wait_send()
        return c

    lax.fori_loop(1, KA, s_done, 0)

    is_red = lax.rem(k, 4) == 1 + core
    t_me = quarter

    r16 = pl.ds(pl.multiple_of(t_me * 16, 16), 16)

    def a_copy(o):
        return pltpu.make_async_remote_copy(
            src_ref=fin_send.at[0], dst_ref=out_hbm.at[r16], send_sem=a_ss.at[o], recv_sem=a_rs,
            device_id=ka_peer(o), device_id_type=MESH)

    def o_copy(o):
        return pltpu.make_async_remote_copy(
            src_ref=fin_send.at[1], dst_ref=sgrad_hbm.at[r16], send_sem=o_ss.at[o], recv_sem=o_rs,
            device_id=ka_peer(o), device_id_type=MESH)

    @pl.when(is_red)
    def _():
        pltpu.make_async_copy(att_recv, att_recv, t_rs).wait()
        att16 = jnp.sum(att_recv[...].astype(F32), axis=0)
        g16 = gate_s[r16, :]
        fin_send[0] = nn((g16 * att16).astype(BF16), weight(O_T)).astype(BF16)

        def a_start(o, c):
            a_copy(o).start()
            return c

        lax.fori_loop(1, KA, a_start, 0)
        pltpu.make_async_copy(fin_send.at[0], out_hbm.at[r16], a_rs).start()
        gig = cot_s[r16, :] * att16 * g16 * (1.0 - g16)
        part = back(gig, G_T)
        pltpu.make_async_copy(qg_recv, qg_recv, q_rs).wait()
        part = part + jnp.sum(qg_recv[...].astype(F32), axis=0)
        pltpu.make_async_copy(kg_recv, kg_recv, k_rs).wait()
        ig = part + jnp.sum(kg_recv[...].astype(F32), axis=0)
        n16 = nsg[r16, :]
        sgr = isg[r16, 0:1] * (
            ig - jnp.mean(ig, axis=-1, keepdims=True) - n16 * jnp.mean(ig * n16, axis=-1, keepdims=True))
        fin_send[1] = sgr.astype(BF16)

        def o_start(o, c):
            o_copy(o).start()
            return c

        lax.fori_loop(1, KA, o_start, 0)
        pltpu.make_async_copy(fin_send.at[1], sgrad_hbm.at[r16], o_rs).start()

    for n in range(4):
        pair_out(n).wait()

    def k_done(t, c):
        @pl.when(jnp.logical_not(k_mine(t)))
        def _():
            k_copy(t).wait_send()

        return c

    lax.fori_loop(0, 4, k_done, 0)
    h_copy.wait_send()

    def q_done(t, c):
        @pl.when(red_of(t) != k)
        def _():
            q_copy(t).wait_send()
            t_copy(t).wait_send()

        return c

    lax.fori_loop(0, 4, q_done, 0)

    @pl.when(is_red)
    def _():
        def o_done(o, c):
            a_copy(o).wait_send()
            o_copy(o).wait_send()
            return c

        lax.fori_loop(1, KA, o_done, 0)

    pltpu.make_async_copy(out_hbm, out_hbm, a_rs).wait()
    pltpu.make_async_copy(sgrad_hbm, sgrad_hbm, o_rs).wait()


def hand_over(out_a, sgrad_a, pgrad_a, out_b, sgrad_b, pgrad_b, out_v, sgrad_v, pgrad_v, in_sem, out_sem):
    parts = [
        (pgrad_a.at[pl.ds(n * 8, 8)], pgrad_v.at[pl.ds(n * 8, 8)], pgrad_b.at[pl.ds(n * 8, 8)]) for n in range(8)
    ]
    parts = [(out_a, out_v, out_b), (sgrad_a, sgrad_v, sgrad_b)] + parts
    for n, (src, mid, _) in enumerate(parts):
        pltpu.make_async_copy(src, mid, in_sem.at[n]).start()
    for n, (src, mid, dst) in enumerate(parts):
        pltpu.make_async_copy(src, mid, in_sem.at[n]).wait()
        pltpu.make_async_copy(mid, dst, out_sem.at[n]).start()
    for n, (_, mid, dst) in enumerate(parts):
        pltpu.make_async_copy(mid, dst, out_sem.at[n]).wait()


def local(*args):
    args = args[:10] + (args[10].T,)
    hbm = pl.BlockSpec(memory_space=pltpu.HBM)
    dma = pltpu.SemaphoreType.DMA
    big = (ROWS, COLS, CP)
    flat = (HEADS * ROWS, 128)
    results = pl.pallas_call(
        kernel,
        out_shape=(
            jax.ShapeDtypeStruct((ROWS, D), BF16),
            jax.ShapeDtypeStruct((ROWS, D), BF16),
            jax.ShapeDtypeStruct(big, BF16),
        ),
        in_specs=[hbm] * 11,
        out_specs=(hbm, hbm, hbm),
        scratch_shapes=[
            pltpu.VMEM(big, BF16),
            pltpu.VMEM((ROWS, D), BF16),
            pltpu.VMEM((COLS,), jnp.int32),
            pltpu.VMEM((ROWS, D), BF16),
            pltpu.VMEM((D,), BF16),
            pltpu.VMEM((HEADS, CP), BF16),
            pltpu.VMEM(big, BF16),
            pltpu.VMEM(big, F32),
            pltpu.VMEM(big, F32),
            pltpu.VMEM(flat, F32),
            pltpu.VMEM(flat, F32),
            pltpu.VMEM((4, 16, D), BF16),
            pltpu.VMEM((ROWS, D), F32),
            pltpu.VMEM((ROWS, 128), F32),
            pltpu.VMEM((2, 4, 16, D), BF16),
            pltpu.VMEM((16, 24, 128), BF16),
            pltpu.VMEM((KA, 16, 24, 128), BF16),
            pltpu.VMEM((16, D, 128), BF16),
            pltpu.VMEM((HEADS * ROWS, D), BF16),
            pltpu.VMEM((HEADS * ROWS, D), BF16),
            pltpu.VMEM((ROWS, D), F32),
            pltpu.VMEM((ROWS, D), F32),
            pltpu.VMEM(flat, F32),
            pltpu.VMEM(flat, F32),
            pltpu.VMEM(flat, BF16),
            pltpu.VMEM(flat, BF16),
            pltpu.VMEM((KA, 24, 128), F32),
            pltpu.VMEM((24, 128), F32),
            pltpu.VMEM((2, ROWS, D), F32),
            pltpu.VMEM((ROWS, D), F32),
            pltpu.VMEM((4, 16, D), BF16),
            pltpu.VMEM((PB // 2, 16, D), BF16),
            pltpu.VMEM((4, 16, D), BF16),
            pltpu.VMEM((KA, 16, D), BF16),
            pltpu.VMEM((4, 16, D), BF16),
            pltpu.VMEM((KA, 16, D), BF16),
            pltpu.VMEM((2, 16, D), BF16),
            dma((4,)), dma((4,)), dma((5,)), dma((16,)),
            dma((16,)), dma, dma, dma,
            dma((15,)), dma((15,)),
            dma((15,)), dma((15,)),
            dma((16,)), dma,
            dma, dma,
            dma((4,)), dma,
            dma((4,)), dma,
            dma((4,)), dma,
            dma((16,)), dma,
            dma((16,)), dma,
        ],
        compiler_params=pltpu.CompilerParams(
            collective_id=0, has_side_effects=True, vmem_limit_bytes=60 * 1024 * 1024),
    )(*args)
    return pl.pallas_call(
        hand_over,
        out_shape=tuple(jax.ShapeDtypeStruct(r.shape, r.dtype) for r in results),
        in_specs=[hbm] * 3,
        out_specs=(hbm,) * 3,
        scratch_shapes=[pltpu.VMEM(r.shape, r.dtype) for r in results] + [dma((10,)), dma((10,))],
        compiler_params=pltpu.CompilerParams(vmem_limit_bytes=60 * 1024 * 1024),
    )(*results)


def solution(mesh):
    in_specs = (
        P("pb", None), P("pb", "ka", None), P("ka"), P("pb", None), P("ka", None), P(),
        P("ka", None), P("ka", None), P("ka", None), P("ka", None), P(),
    )
    out_specs = (P("pb", None), P("pb", None), P("pb", "ka", None))
    return jax.shard_map(local, mesh=mesh, in_specs=in_specs, out_specs=out_specs, check_vma=False)
```

```python
import functools

import jax
import jax.numpy as jnp
from jax import lax
from jax.experimental import pallas as pl
from jax.experimental.pallas import tpu as pltpu
from jax.sharding import PartitionSpec as P

MESH = pl.DeviceIdType.MESH
F32 = jnp.float32
BF16 = jnp.bfloat16
EPS = 1e-05
PENALTY = 1000000000.0

ROWS = 64
COLS = 128
HEADS = 16
DIM = 24
D = 384
CP = 128
KA = 16
PB = 32
SCALE = DIM ** (-0.5)
K_T, Q_T, V_T, G_T, O_T = (0, 1, 2), (3, 4, 5), (8, 9, 10), (11, 12, 13), (6, 7, 14)
NEAR = [(a, b) for a in range(4) for b in ((0, 1, -1, 2) if a % 2 == 0 else (0, 1, -1, -2)) if (a, b) != (0, 0)]
NEAR.sort(key=lambda o: min(o[0], 4 - o[0]) + abs(o[1]))


def nt(a, b):
    return lax.dot_general(a, b, (((1,), (1,)), ((), ())), preferred_element_type=F32)


def tn(a, b):
    return lax.dot_general(a, b, (((0,), (0,)), ((), ())), preferred_element_type=F32)


def nn(a, b):
    return jnp.dot(a, b, preferred_element_type=F32)


def split2(v):
    hi = v.astype(BF16)
    return hi, (v - hi.astype(F32)).astype(BF16)


def kernel(
    single_hbm, pair_hbm, mask_hbm, ocot_hbm, wq_hbm, qb_hbm, wk_hbm, wv_hbm, wg_hbm, wo_hbm, pw_hbm,
    out_hbm, sgrad_hbm, pgrad_hbm,
    outb,    single_ref, mask_ref, ocot_ref, qb_ref, pw_ref, xp, nrm, invb, bias, sgp, a_i, nsg, isg, xall, wsend, wall, wfull, qbig, gbig, gate_s, cot_s,
    ebuf, dpbuf, sgb, pbb, stats, stat_send, kv_half, kv_other, kg_send, kg_recv, att_send, att_recv, qg_send, qg_recv, fin_send,
    in_sem, out_sem, small_sem, wl_sem, x_ss, x_rs, xf_ss, xf_rs, w_ss, w_rs, f_ss, f_rs, s_ss, s_rs, h_ss, h_rs, k_ss, k_rs, t_ss, t_rs, q_ss, q_rs, a_ss, a_rs, o_ss, o_rs,
):
    p = lax.axis_index("pb")
    k = lax.axis_index("ka")
    core = lax.rem(p, 2)
    y = lax.rem(lax.div(p, 2), 8)
    x = lax.div(k, 4)
    z = lax.div(p, 16) * 4 + lax.rem(k, 4)
    sib = (p + 1 - 2 * core, k)
    own = lax.div(p, 2)
    quarter = lax.div(k, 4)
    rgroup = lax.rem(k, 4)
    chip = lax.div(p, 2)

    def at(x2, z2):
        x2 = lax.rem(x2 + 4, 4)
        z2 = lax.rem(z2 + 8, 8)
        return ((lax.div(z2, 4) * 8 + y) * 2 + core, x2 * 4 + lax.rem(z2, 4))

    def ka_peer(o):
        return (p, lax.rem(k + o, KA))

    def x_target(o):
        return (lax.rem(chip + o, 16) * 2 + core, own)

    def x_source(o):
        return (2 * k + core, quarter * 4 + o)

    def pair_in(n):
        return pltpu.make_async_copy(pair_hbm.at[pl.ds(n * 16, 16)], xp.at[pl.ds(n * 16, 16)], in_sem.at[n])


    bar = pltpu.get_barrier_semaphore()

    def greet_x(o, c):
        src = x_source(o)

        @pl.when(jnp.logical_or(src[0] != p, src[1] != k))
        def _():
            pl.semaphore_signal(bar, inc=1, device_id=src, device_id_type=MESH)

        return c

    lax.fori_loop(0, 4, greet_x, 0)

    def greet_ka(o, c):
        pl.semaphore_signal(bar, inc=1, device_id=ka_peer(o), device_id_type=MESH)
        return c

    lax.fori_loop(1, KA, greet_ka, 0)
    for a, b in NEAR:
        pl.semaphore_signal(bar, inc=1, device_id=at(x - a, z - b), device_id_type=MESH)
    pl.semaphore_signal(bar, inc=1, device_id=sib, device_id_type=MESH)

    single_in = pltpu.make_async_copy(single_hbm, single_ref, small_sem.at[0])
    single_in.start()
    weights_in = [
        pltpu.make_async_copy(ref.at[:, pl.ds(n * 128, 128)], wsend.at[t], wl_sem.at[t])
        for ref, tiles in ((wk_hbm, K_T), (wq_hbm, Q_T), (wv_hbm, V_T), (wg_hbm, G_T), (wo_hbm, O_T))
        for n, t in enumerate(tiles)
    ]
    for copy in weights_in:
        copy.start()
    small_in = [
        pltpu.make_async_copy(src, dst, small_sem.at[n + 1])
        for n, (src, dst) in enumerate(((mask_hbm, mask_ref), (ocot_hbm, ocot_ref), (qb_hbm, qb_ref), (pw_hbm, pw_ref)))
    ]
    for copy in small_in:
        copy.start()
    for n in range(4):
        pair_in(n).start()
    single_in.wait()
    sv = single_ref[...].astype(F32)
    cen = sv - jnp.mean(sv, axis=-1, keepdims=True)
    inv = lax.rsqrt(jnp.mean(cen * cen, axis=-1, keepdims=True) + EPS)
    normed = cen * inv
    nsg[...] = normed
    isg[...] = jnp.broadcast_to(inv, (ROWS, 128))
    a_i[...] = normed.astype(BF16).reshape(4, 16, D)

    for copy in weights_in:
        copy.wait()
    wsend[15] = jnp.zeros((24, 128), BF16)
    wall[k] = wsend[...]

    self_x = own == k
    x_sends = lax.div(own, 4) == quarter
    pl.semaphore_wait(bar, 15 + 15 + 1 + 16 * x_sends.astype(jnp.int32) - self_x.astype(jnp.int32))

    def x_copy(o):
        return pltpu.make_async_remote_copy(
            src_ref=a_i.at[rgroup], dst_ref=xall.at[core, rgroup], send_sem=x_ss.at[o], recv_sem=x_rs,
            device_id=x_target(o), device_id_type=MESH)

    def x_self():
        return pltpu.make_async_copy(a_i.at[rgroup], xall.at[core, rgroup], x_rs)

    @pl.when(self_x)
    def _():
        x_self().start()

    @pl.when(jnp.logical_and(x_sends, jnp.logical_not(self_x)))
    def _():
        x_copy(0).start()

    @pl.when(x_sends)
    def _():
        def x_send(o, c):
            x_copy(o).start()
            return c

        lax.fori_loop(1, 16, x_send, 0)

    half = pl.ds(core * 8, 8)

    def w_copy(o):
        a, b = NEAR[o]
        return pltpu.make_async_remote_copy(
            src_ref=wsend.at[half], dst_ref=wall.at[k, half], send_sem=w_ss.at[o], recv_sem=w_rs.at[o],
            device_id=at(x + a, z + b), device_id_type=MESH)

    for o in range(15):
        w_copy(o).start()

    for copy in small_in:
        copy.wait()
    pwt_b = pw_ref[...]
    pwt = pwt_b.astype(F32)

    mean_w = jnp.full((CP, CP), 1.0 / CP, BF16)

    def pair_body(n, c):
        i8 = pl.ds(pl.multiple_of(n * 8, 8), 8)
        vb = xp[i8].reshape(8 * COLS, CP)
        v = vb.astype(F32)
        cv = v - nn(vb, mean_w)
        sq_hi, sq_lo = split2(cv * cv)
        iv = lax.rsqrt(nn(sq_hi, mean_w) + nn(sq_lo, mean_w) + EPS)
        nv = cv * iv
        nrm[i8] = nv.reshape(8, COLS, CP)
        invb[i8] = iv.reshape(8, COLS, CP)
        hi, mid = split2(nv)
        both = nt(pwt_b, hi) + nt(pwt_b, mid)
        for m in range(8):
            bias[pl.ds(pl.multiple_of(n * 128 + m * 16, 16), 16), :] = both[:, m * 128 : (m + 1) * 128]
        return c

    def f_copy(o):
        a, b = NEAR[o]
        src = at(x - a, z - b)[1]
        return pltpu.make_async_remote_copy(
            src_ref=wall.at[src, half], dst_ref=wall.at[src, half], send_sem=f_ss.at[o], recv_sem=f_rs.at[o],
            device_id=sib, device_id_type=MESH)

    for n in range(4):
        pair_in(n).wait()
        lax.fori_loop(n * 2, n * 2 + 2, pair_body, 0)
        if n == 2:
            for o in range(6):
                w_copy(o).wait_recv()
                f_copy(o).start()

    for o in range(6, 15):
        w_copy(o).wait_recv()
        f_copy(o).start()

    pltpu.make_async_copy(xall.at[core], xall.at[core], x_rs).wait()
    x_fwd = pltpu.make_async_remote_copy(
        src_ref=xall.at[core], dst_ref=xall.at[core], send_sem=xf_ss, recv_sem=xf_rs,
        device_id=sib, device_id_type=MESH)
    x_fwd.start()

    def build(first):
        for n in range(8):
            wfull[first + n] = wall[:, first + n].astype(F32).reshape(D, 128).astype(BF16)

    build(core * 8)
    for o in range(15):
        f_copy(o).wait_recv()
    build(8 - core * 8)
    x_fwd.wait_recv()

    def weight(tiles):
        return jnp.concatenate([wfull[t] for t in tiles], axis=1)

    keys_in = xall[...].reshape(COLS, D)
    rows_in = a_i[...].reshape(ROWS, D)
    keys = nn(keys_in, weight(K_T)).astype(BF16)
    values = nn(keys_in, weight(V_T)).astype(BF16)
    queries = (nn(rows_in, weight(Q_T)) + qb_ref[...].astype(F32).reshape(1, D)).astype(BF16)
    gate = jax.nn.sigmoid(nn(rows_in, weight(G_T)))
    cot = nt(ocot_ref[...], weight(O_T))
    gate_s[...] = gate
    cot_s[...] = cot
    agrad = (gate * cot).astype(BF16)

    lane_head = lax.div(lax.broadcasted_iota(jnp.int32, (1, D), 1), DIM)
    heads_f = [jnp.where(lane_head == h, 1.0, 0.0).astype(F32) for h in range(HEADS)]
    for h in range(HEADS):
        mask_b = heads_f[h].astype(BF16)
        qbig[h * ROWS : (h + 1) * ROWS, :] = queries * mask_b
        gbig[h * ROWS : (h + 1) * ROWS, :] = agrad * mask_b

    pen = (mask_ref[...].astype(F32).reshape(1, COLS) - 1.0) * PENALTY
    lane = lax.broadcasted_iota(jnp.int32, (8, 128), 1)
    pm = jnp.zeros((8, 128), F32)
    pt = jnp.zeros((8, 128), F32)
    pd = jnp.zeros((8, 128), F32)
    for h in range(HEADS):
        rows = slice(h * ROWS, (h + 1) * ROWS)
        logits = nt(qbig[rows, :], keys) * SCALE + bias[pl.ds(h, ROWS, stride=HEADS), :] + pen
        dp = nt(gbig[rows, :], values)
        mx = jnp.max(logits, axis=-1, keepdims=True)
        e = jnp.exp(logits - mx)
        ebuf[rows, :] = e
        dpbuf[rows, :] = dp
        tot = jnp.sum(e, axis=-1, keepdims=True)
        dd = jnp.sum(e * dp, axis=-1, keepdims=True)
        for g in range(8):
            here = lane == g * 16 + h
            s8 = slice(g * 8, g * 8 + 8)
            pm = jnp.where(here, mx[s8], pm)
            pt = jnp.where(here, tot[s8], pt)
            pd = jnp.where(here, dd[s8], pd)
    stat_send[0:8, :] = pm
    stat_send[8:16, :] = pt
    stat_send[16:24, :] = pd

    def s_copy(o):
        return pltpu.make_async_remote_copy(
            src_ref=stat_send, dst_ref=stats.at[k], send_sem=s_ss.at[o], recv_sem=s_rs,
            device_id=ka_peer(o), device_id_type=MESH)

    def s_start(o, c):
        s_copy(o).start()
        return c

    lax.fori_loop(1, KA, s_start, 0)
    pltpu.make_async_copy(stat_send, stats.at[k], s_rs).start()
    num = jnp.zeros((ROWS, D), F32)
    for h in range(HEADS):
        rows = slice(h * ROWS, (h + 1) * ROWS)
        num = num + nn(ebuf[rows, :].astype(BF16), values) * heads_f[h]
    pltpu.make_async_copy(stats, stats, s_rs).wait()

    st = stats[...]
    all_m, all_t, all_d = st[:, 0:8], st[:, 8:16], st[:, 16:24]
    gm = jnp.max(all_m, axis=0)
    wts = jnp.exp(all_m - gm[None])
    gt = jnp.sum(wts * all_t, axis=0)
    gd = jnp.sum(wts * all_d, axis=0)
    coef = jnp.exp(pm - gm) / gt
    delta = gd / gt
    coef_f = jnp.zeros((ROWS, D), F32)
    for h in range(HEADS):
        cc = jnp.concatenate([jnp.broadcast_to(coef[:, g * 16 + h : g * 16 + h + 1], (8, 128)) for g in range(8)], axis=0)
        coef_f = coef_f + jnp.concatenate([cc] * 3, axis=1) * heads_f[h]
    att_send[...] = (num * coef_f).astype(BF16).reshape(4, 16, D)

    def red_of(t):
        return 4 * t + 1 + core

    def t_copy(t):
        return pltpu.make_async_remote_copy(
            src_ref=att_send.at[t], dst_ref=att_recv.at[k], send_sem=t_ss.at[t], recv_sem=t_rs,
            device_id=(p, red_of(t)), device_id_type=MESH)

    def t_start(t, c):
        mine = red_of(t) == k

        @pl.when(mine)
        def _():
            pltpu.make_async_copy(att_send.at[t], att_recv.at[k], t_rs).start()

        @pl.when(jnp.logical_not(mine))
        def _():
            t_copy(t).start()

        return c

    lax.fori_loop(0, 4, t_start, 0)

    for h in range(HEADS):
        rows = slice(h * ROWS, (h + 1) * ROWS)
        cc = jnp.concatenate([jnp.broadcast_to(coef[:, g * 16 + h : g * 16 + h + 1], (8, 128)) for g in range(8)], axis=0)
        dc = jnp.concatenate([jnp.broadcast_to(delta[:, g * 16 + h : g * 16 + h + 1], (8, 128)) for g in range(8)], axis=0)
        prob = ebuf[rows, :] * cc
        sg = prob * (dpbuf[rows, :] - dc)
        sgp[pl.ds(h, ROWS, stride=HEADS), :] = sg
        sgb[rows, :] = sg.astype(BF16)
        pbb[rows, :] = prob.astype(BF16)

    def back(v, n):
        hi, lo = split2(v)
        w = weight(n)
        return nt(hi, w) + nt(lo, w)

    key_in = nt((tn(sgb[...], qbig[...]) * SCALE).astype(BF16), weight(K_T)) + nt(
        tn(pbb[...], gbig[...]).astype(BF16), weight(V_T))
    kv_half[0] = key_in[0:ROWS]
    kv_half[1] = key_in[ROWS : 2 * ROWS]
    h_copy = pltpu.make_async_remote_copy(
        src_ref=kv_half.at[1 - core], dst_ref=kv_other, send_sem=h_ss, recv_sem=h_rs,
        device_id=sib, device_id_type=MESH)
    h_copy.start()

    qg = jnp.zeros((ROWS, D), F32)
    for h in range(HEADS):
        rows = slice(h * ROWS, (h + 1) * ROWS)
        qg = qg + nn(sgb[rows, :], keys) * heads_f[h]
    row_in = nt((qg * SCALE).astype(BF16), weight(Q_T))
    qg_send[...] = row_in.astype(BF16).reshape(4, 16, D)

    def q_copy(t):
        return pltpu.make_async_remote_copy(
            src_ref=qg_send.at[t], dst_ref=qg_recv.at[k], send_sem=q_ss.at[t], recv_sem=q_rs,
            device_id=(p, red_of(t)), device_id_type=MESH)

    def q_start(t, c):
        mine = red_of(t) == k

        @pl.when(mine)
        def _():
            pltpu.make_async_copy(qg_send.at[t], qg_recv.at[k], q_rs).start()

        @pl.when(jnp.logical_not(mine))
        def _():
            q_copy(t).start()

        return c

    lax.fori_loop(0, 4, q_start, 0)

    h_copy.wait_recv()
    kg_send[...] = (kv_half[core] + kv_other[...]).astype(BF16).reshape(4, 16, D)

    def k_copy(t):
        return pltpu.make_async_remote_copy(
            src_ref=kg_send.at[t], dst_ref=kg_recv.at[chip], send_sem=k_ss.at[t], recv_sem=k_rs,
            device_id=(2 * k + core, red_of(t)), device_id_type=MESH)

    def k_mine(t):
        return jnp.logical_and(2 * k + core == p, red_of(t) == k)

    def k_start(t, c):
        mine = k_mine(t)

        @pl.when(mine)
        def _():
            pltpu.make_async_copy(kg_send.at[t], kg_recv.at[chip], k_rs).start()

        @pl.when(jnp.logical_not(mine))
        def _():
            k_copy(t).start()

        return c

    lax.fori_loop(0, 4, k_start, 0)

    wc = pwt - jnp.mean(pwt, axis=-1, keepdims=True)
    wc_hi, wc_lo = split2(wc)
    zero16 = jnp.zeros((16, 128), BF16)
    ones8 = jnp.where(lax.broadcasted_iota(jnp.int32, (16, 128), 0) < 2, 1.0, 0.0).astype(BF16)
    rhs = jnp.concatenate(
        [jnp.concatenate([wc_hi, wc_hi, wc_lo, zero16], axis=0), jnp.concatenate([zero16, zero16, zero16, ones8], axis=0)], axis=1)
    row16 = lax.broadcasted_iota(jnp.int32, (16, 128), 0)

    def grad_body(i, c):
        r16 = pl.ds(pl.multiple_of(i * 16, 16), 16)
        sg = sgp[r16, :]
        s = jnp.sum(sg * bias[r16, :], axis=0, keepdims=True) * (1.0 / CP)
        hi, lo = split2(sg)
        s_hi = s.astype(BF16).astype(F32)
        s2 = jnp.where(row16 == 0, s_hi, jnp.where(row16 == 1, s - s_hi, 0.0)).astype(BF16)
        lhs = jnp.concatenate([hi, lo, hi, s2], axis=0)
        both = tn(lhs, rhs)
        outb[i] = (invb[i] * (both[:, :128] - nrm[i] * both[:, 128:])).astype(BF16)
        return c

    def pair_out(n):
        return pltpu.make_async_copy(outb.at[pl.ds(n * 16, 16)], pgrad_hbm.at[pl.ds(n * 16, 16)], out_sem.at[n])

    for n in range(4):
        lax.fori_loop(n * 16, (n + 1) * 16, grad_body, 0, unroll=4)
        pair_out(n).start()

    x_fwd.wait_send()

    @pl.when(jnp.logical_and(x_sends, jnp.logical_not(self_x)))
    def _():
        x_copy(0).wait_send()

    @pl.when(x_sends)
    def _():
        def x_done(o, c):
            x_copy(o).wait_send()
            return c

        lax.fori_loop(1, 16, x_done, 0)

    for o in range(15):
        w_copy(o).wait_send()
        f_copy(o).wait_send()

    def s_done(o, c):
        s_copy(o).wait_send()
        return c

    lax.fori_loop(1, KA, s_done, 0)

    is_red = lax.rem(k, 4) == 1 + core
    t_me = quarter

    r16 = pl.ds(pl.multiple_of(t_me * 16, 16), 16)

    def a_copy(o):
        return pltpu.make_async_remote_copy(
            src_ref=fin_send.at[0], dst_ref=out_hbm.at[r16], send_sem=a_ss.at[o], recv_sem=a_rs,
            device_id=ka_peer(o), device_id_type=MESH)

    def o_copy(o):
        return pltpu.make_async_remote_copy(
            src_ref=fin_send.at[1], dst_ref=sgrad_hbm.at[r16], send_sem=o_ss.at[o], recv_sem=o_rs,
            device_id=ka_peer(o), device_id_type=MESH)

    @pl.when(is_red)
    def _():
        pltpu.make_async_copy(att_recv, att_recv, t_rs).wait()
        att16 = jnp.sum(att_recv[...].astype(F32), axis=0)
        g16 = gate_s[r16, :]
        fin_send[0] = nn((g16 * att16).astype(BF16), weight(O_T)).astype(BF16)

        def a_start(o, c):
            a_copy(o).start()
            return c

        lax.fori_loop(1, KA, a_start, 0)
        pltpu.make_async_copy(fin_send.at[0], out_hbm.at[r16], a_rs).start()
        gig = cot_s[r16, :] * att16 * g16 * (1.0 - g16)
        part = back(gig, G_T)
        pltpu.make_async_copy(qg_recv, qg_recv, q_rs).wait()
        part = part + jnp.sum(qg_recv[...].astype(F32), axis=0)
        pltpu.make_async_copy(kg_recv, kg_recv, k_rs).wait()
        ig = part + jnp.sum(kg_recv[...].astype(F32), axis=0)
        n16 = nsg[r16, :]
        sgr = isg[r16, 0:1] * (
            ig - jnp.mean(ig, axis=-1, keepdims=True) - n16 * jnp.mean(ig * n16, axis=-1, keepdims=True))
        fin_send[1] = sgr.astype(BF16)

        def o_start(o, c):
            o_copy(o).start()
            return c

        lax.fori_loop(1, KA, o_start, 0)
        pltpu.make_async_copy(fin_send.at[1], sgrad_hbm.at[r16], o_rs).start()

    for n in range(4):
        pair_out(n).wait()

    def k_done(t, c):
        @pl.when(jnp.logical_not(k_mine(t)))
        def _():
            k_copy(t).wait_send()

        return c

    lax.fori_loop(0, 4, k_done, 0)
    h_copy.wait_send()

    def q_done(t, c):
        @pl.when(red_of(t) != k)
        def _():
            q_copy(t).wait_send()
            t_copy(t).wait_send()

        return c

    lax.fori_loop(0, 4, q_done, 0)

    @pl.when(is_red)
    def _():
        def o_done(o, c):
            a_copy(o).wait_send()
            o_copy(o).wait_send()
            return c

        lax.fori_loop(1, KA, o_done, 0)

    pltpu.make_async_copy(out_hbm, out_hbm, a_rs).wait()
    pltpu.make_async_copy(sgrad_hbm, sgrad_hbm, o_rs).wait()


def hand_over(out_a, sgrad_a, pgrad_a, out_b, sgrad_b, pgrad_b, out_v, sgrad_v, pgrad_v, in_sem, out_sem):
    parts = [
        (pgrad_a.at[pl.ds(n * 8, 8)], pgrad_v.at[pl.ds(n * 8, 8)], pgrad_b.at[pl.ds(n * 8, 8)]) for n in range(8)
    ]
    parts = [(out_a, out_v, out_b), (sgrad_a, sgrad_v, sgrad_b)] + parts
    for n, (src, mid, _) in enumerate(parts):
        pltpu.make_async_copy(src, mid, in_sem.at[n]).start()
    for n, (src, mid, dst) in enumerate(parts):
        pltpu.make_async_copy(src, mid, in_sem.at[n]).wait()
        pltpu.make_async_copy(mid, dst, out_sem.at[n]).start()
    for n, (_, mid, dst) in enumerate(parts):
        pltpu.make_async_copy(mid, dst, out_sem.at[n]).wait()


def local(*args):
    args = args[:10] + (args[10].T,)
    hbm = pl.BlockSpec(memory_space=pltpu.HBM)
    dma = pltpu.SemaphoreType.DMA
    big = (ROWS, COLS, CP)
    flat = (HEADS * ROWS, 128)
    results = pl.pallas_call(
        kernel,
        out_shape=(
            jax.ShapeDtypeStruct((ROWS, D), BF16),
            jax.ShapeDtypeStruct((ROWS, D), BF16),
            jax.ShapeDtypeStruct(big, BF16),
        ),
        in_specs=[hbm] * 11,
        out_specs=(hbm, hbm, hbm),
        scratch_shapes=[
            pltpu.VMEM(big, BF16),
            pltpu.VMEM((ROWS, D), BF16),
            pltpu.VMEM((COLS,), jnp.int32),
            pltpu.VMEM((ROWS, D), BF16),
            pltpu.VMEM((D,), BF16),
            pltpu.VMEM((HEADS, CP), BF16),
            pltpu.VMEM(big, BF16),
            pltpu.VMEM(big, F32),
            pltpu.VMEM(big, F32),
            pltpu.VMEM(flat, F32),
            pltpu.VMEM(flat, F32),
            pltpu.VMEM((4, 16, D), BF16),
            pltpu.VMEM((ROWS, D), F32),
            pltpu.VMEM((ROWS, 128), F32),
            pltpu.VMEM((2, 4, 16, D), BF16),
            pltpu.VMEM((16, 24, 128), BF16),
            pltpu.VMEM((KA, 16, 24, 128), BF16),
            pltpu.VMEM((16, D, 128), BF16),
            pltpu.VMEM((HEADS * ROWS, D), BF16),
            pltpu.VMEM((HEADS * ROWS, D), BF16),
            pltpu.VMEM((ROWS, D), F32),
            pltpu.VMEM((ROWS, D), F32),
            pltpu.VMEM(flat, F32),
            pltpu.VMEM(flat, F32),
            pltpu.VMEM(flat, BF16),
            pltpu.VMEM(flat, BF16),
            pltpu.VMEM((KA, 24, 128), F32),
            pltpu.VMEM((24, 128), F32),
            pltpu.VMEM((2, ROWS, D), F32),
            pltpu.VMEM((ROWS, D), F32),
            pltpu.VMEM((4, 16, D), BF16),
            pltpu.VMEM((PB // 2, 16, D), BF16),
            pltpu.VMEM((4, 16, D), BF16),
            pltpu.VMEM((KA, 16, D), BF16),
            pltpu.VMEM((4, 16, D), BF16),
            pltpu.VMEM((KA, 16, D), BF16),
            pltpu.VMEM((2, 16, D), BF16),
            dma((4,)), dma((4,)), dma((5,)), dma((16,)),
            dma((16,)), dma, dma, dma,
            dma((15,)), dma((15,)),
            dma((15,)), dma((15,)),
            dma((16,)), dma,
            dma, dma,
            dma((4,)), dma,
            dma((4,)), dma,
            dma((4,)), dma,
            dma((16,)), dma,
            dma((16,)), dma,
        ],
        compiler_params=pltpu.CompilerParams(
            collective_id=0, has_side_effects=True, vmem_limit_bytes=60 * 1024 * 1024),
    )(*args)
    return pl.pallas_call(
        hand_over,
        out_shape=tuple(jax.ShapeDtypeStruct(r.shape, r.dtype) for r in results),
        in_specs=[hbm] * 3,
        out_specs=(hbm,) * 3,
        scratch_shapes=[pltpu.VMEM(r.shape, r.dtype) for r in results] + [dma((10,)), dma((10,))],
        compiler_params=pltpu.CompilerParams(vmem_limit_bytes=60 * 1024 * 1024),
    )(*results)


def solution(mesh):
    in_specs = (
        P("pb", None), P("pb", "ka", None), P("ka"), P("pb", None), P("ka", None), P(),
        P("ka", None), P("ka", None), P("ka", None), P("ka", None), P(),
    )
    out_specs = (P("pb", None), P("pb", None), P("pb", "ka", None))
    return jax.shard_map(local, mesh=mesh, in_specs=in_specs, out_specs=out_specs, check_vma=False)
```
